256 devices in a mesh: dp: 4 (over z_hi, core), grid: 64 (over x, z_lo, y).
Axes of the slice: x: 4, y: 4, z: 8 (z_hi: 2, z_lo: 4; z = z_hi * 4 + z_lo), core: 2. Of those that a mesh axis runs over, the one named last changes fastest.
Arguments:
- snapshots: bfloat16 [4, 64, 128, 64, 128], P('dp', None, 'grid'), may hold values from -6 to 6
- cotangent: bfloat16 [4, 32, 128, 64, 128], P('dp', None, 'grid'), may hold values from -6 to 6
- local_weight: bfloat16 [64, 32], replicated, may hold values from -0.75 to 0.75
- spectral_weight: float32 [32, 512, 4096], P('dp', 'grid'), may hold values from -6 to 6
- first_moment: float32 [32, 512, 4096], P('dp', 'grid'), may hold values from -6 to 6
- second_moment: float32 [32, 512, 4096], P('dp', 'grid'), may hold values from 1 to 30
Outputs:
- grad_input: bfloat16 [4, 64, 128, 64, 128], P('dp', None, 'grid')
- local_grad: float32 [64, 32], replicated
- new_weight: float32 [32, 512, 4096], P('dp', 'grid')
- new_first: float32 [32, 512, 4096], P('dp', 'grid')
- new_second: float32 [32, 512, 4096], P('dp', 'grid')
The draws below stay inside these ranges and needn't reach their ends.
All inputs are finite; a program needn't handle non-finite values.
Results may differ from the reference program's by a relative error of at most 0.0056.
Values sent between devices are 32-bit elements; how exact they have to be, the bound alone decides.
A program may use at most 128 MiB of HBM per device.

```python
import math
import jax
import jax.numpy as jnp
from jax import lax

C = 64
CO = 32
NX = 128
NY = 64
NZ = 128
KX = 32
KY = 32
KZ = 16
STEP = 100
SNAPS = 4


def levels(rng, dims, pieces, smallest, high):
    level = 1.0
    for dim, parts in pieces:
        steps = jax.random.uniform(jax.random.fold_in(jax.random.fold_in(rng, 6), dim), (parts,), jnp.float32, smallest / len(pieces), high / len(pieces))
        level = level * jnp.repeat(jnp.exp(steps), dims[dim] // parts).reshape((-1,) + (1,) * (len(dims) - 1 - dim))
    return level


def noise(stream_key, dims, width, bound, shards=(), held_as=jnp.bfloat16):
    entries = width * jax.random.normal(stream_key, dims, jnp.float32)
    if shards:
        entries = entries * levels(stream_key, dims, shards, -0.22, 0.18)
    return jnp.clip(entries, -bound, bound).astype(held_as)


def setup_inputs(seed: int = 0) -> dict:
    arg_keys = jax.random.split(jax.random.key(seed), 7)
    snapshots = noise(arg_keys[0], (SNAPS, C, NX, NY, NZ), 1.0, 6.0, ((0, 4), (2, 64)))
    cotangent = noise(arg_keys[1], (SNAPS, CO, NX, NY, NZ), 1.0, 6.0, ((0, 4), (2, 64)))
    local_weight = noise(arg_keys[2], (C, CO), C ** -0.5, 0.75)
    spectral_weight = noise(arg_keys[3], (KX, KY * KZ, 2 * C * CO), 0.7, 6.0, ((0, 4), (1, 64)), jnp.float32)
    first_moment = noise(arg_keys[4], (KX, KY * KZ, 2 * C * CO), 2.0, 6.0, ((0, 4), (1, 64)), jnp.float32)
    second_moment = jnp.clip(jnp.exp(math.log(30.0) - 3.4011974 * jax.random.uniform(arg_keys[5], (KX, KY * KZ, 2 * C * CO), jnp.float32) ** levels(arg_keys[5], (KX, KY * KZ, 2 * C * CO), ((0, 4), (1, 64)), -0.2, 0.2)), 1.0, 30.0)
    return dict(snapshots=snapshots, cotangent=cotangent, local_weight=local_weight, spectral_weight=spectral_weight, first_moment=first_moment, second_moment=second_moment)


highest = lax.Precision.HIGHEST
learning_rate = 0.02

def mode_numbers(length, retained):
    indices = jnp.arange(retained, dtype=jnp.int32)
    return jnp.where(indices < retained // 2, indices, length - retained + indices)

def phase_table(length, numbers):
    points = jnp.arange(length, dtype=jnp.int32)
    windings = points[:, None] * numbers[None, :] % length
    return windings.astype(jnp.float32) * (2.0 * math.pi / length)

def rotation(angles, direction, scaling):
    cosine = jnp.cos(angles) * scaling
    sine_part = direction * jnp.sin(angles) * scaling
    return jnp.stack([jnp.stack([cosine, sine_part]), jnp.stack([-sine_part, cosine])])

def forward_tables(z_scale):
    z_angles = phase_table(NZ, jnp.arange(KZ, dtype=jnp.int32))
    z_table = jnp.stack([jnp.cos(z_angles) * z_scale[None, :], -jnp.sin(z_angles) * z_scale[None, :]], axis=1).astype(jnp.bfloat16)
    y_table = rotation(phase_table(NY, mode_numbers(NY, KY)), -1.0, 1.0)
    x_table = rotation(phase_table(NX, mode_numbers(NX, KX)), -1.0, 1.0)
    return (z_table, y_table, x_table)

def inverse_tables(z_scale):
    x_table = rotation(phase_table(NX, mode_numbers(NX, KX)).T, 1.0, 1.0)
    y_table = rotation(phase_table(NY, mode_numbers(NY, KY)).T, 1.0, 1.0)
    z_angles = phase_table(NZ, jnp.arange(KZ, dtype=jnp.int32)).T
    z_table = jnp.stack([z_scale[:, None] * jnp.cos(z_angles), -z_scale[:, None] * jnp.sin(z_angles)])
    return (x_table, y_table, z_table)

def forward_modes(values, tables):
    z_table, y_table, x_table = tables
    partial_z = jnp.einsum('ncxyz,zrq->nrqcxy', values.astype(jnp.float32), z_table.astype(jnp.float32), precision=highest)
    partial_y = jnp.einsum('nrqcxy,rsyk->nsxkqc', partial_z, y_table, precision=highest)
    snapshot_count = partial_y.shape[0]
    channel_count = partial_y.shape[-1]
    shaped = partial_y.reshape(snapshot_count, 2, NX, KY * KZ, channel_count)
    return jnp.einsum('nsxmc,stxk->ntkmc', shaped, x_table, precision=highest)

def inverse_modes(spectra, tables):
    x_table, y_table, z_table = tables
    along_x = jnp.einsum('nrkmo,rskx->nsxmo', spectra, x_table, precision=highest)
    snapshot_count = along_x.shape[0]
    channel_count = along_x.shape[-1]
    shaped = along_x.reshape(snapshot_count, 2, NX, KY, KZ, channel_count)
    along_y = jnp.einsum('nrxkqo,rsky->nsxyqo', shaped, y_table, precision=highest)
    return jnp.einsum('nrxyqo,rqz->noxyz', along_y, z_table, precision=highest)

def mix_modes(spectra, weights):

    def product(left_part, right_part):
        return jnp.einsum('nkmi,kmio->nkmo', left_part, right_part, precision=highest)
    real_part = product(spectra[:, 0], weights[:, :, 0]) - product(spectra[:, 1], weights[:, :, 1])
    imag_part = product(spectra[:, 0], weights[:, :, 1]) + product(spectra[:, 1], weights[:, :, 0])
    return jnp.stack([real_part, imag_part], axis=1)

def weight_grads(spectra, gradients):

    def outer_product(left_part, right_part):
        return jnp.einsum('nkmi,nkmo->kmio', left_part, right_part, precision=highest)
    real_part = outer_product(spectra[:, 0], gradients[:, 0]) + outer_product(spectra[:, 1], gradients[:, 1])
    imag_part = outer_product(spectra[:, 0], gradients[:, 1]) - outer_product(spectra[:, 1], gradients[:, 0])
    return jnp.stack([real_part, imag_part], axis=2)

def input_grads(weights, gradients):

    def contract(right_part, left_part):
        return jnp.einsum('kmio,nkmo->nkmi', right_part, left_part, precision=highest)
    real_part = contract(weights[:, :, 0], gradients[:, 0]) + contract(weights[:, :, 1], gradients[:, 1])
    imag_part = contract(weights[:, :, 0], gradients[:, 1]) - contract(weights[:, :, 1], gradients[:, 0])
    return jnp.stack([real_part, imag_part], axis=1)

def gelu_tanh(values):
    return jax.nn.gelu(values, approximate=True)

def adam_update(weight, first_moment, second_moment, gradients):
    new_first = 0.9 * first_moment + 0.1 * gradients
    new_second = 0.999 * second_moment + 0.001 * gradients * gradients
    corrected_first = new_first / (1.0 - 0.9 ** STEP)
    corrected_second = new_second / (1.0 - 0.999 ** STEP)
    new_weight = weight - learning_rate * corrected_first / (jnp.sqrt(corrected_second) + 1e-08)
    return (new_weight, new_first, new_second)

def reference(snapshots, cotangent, local_weight, spectral_weight, first_moment, second_moment):
    weights = spectral_weight.reshape(KX, KY * KZ, 2, C, CO)
    kz_numbers = jnp.arange(KZ, dtype=jnp.int32)
    unit_scale = jnp.ones((KZ,), jnp.float32)
    fold_scale = jnp.where(kz_numbers == 0, 1.0, 2.0).astype(jnp.float32) / (NX * NY * NZ)
    forward_plain = forward_tables(unit_scale)
    forward_scaled = forward_tables(fold_scale)
    inverse_scaled = inverse_tables(fold_scale)
    inverse_plain = inverse_tables(unit_scale)
    local_f32 = local_weight.astype(jnp.float32)

    def one_snapshot(running, current):
        values = current[0][None]
        cot_values = current[1][None]
        spectra = forward_modes(values, forward_plain)
        mixed = mix_modes(spectra, weights)
        pre_act = inverse_modes(mixed, inverse_scaled) + jnp.einsum('ncxyz,co->noxyz', values.astype(jnp.float32), local_f32, precision=highest)
        _, backward = jax.vjp(gelu_tanh, pre_act)
        pre_grad = backward(cot_values.astype(jnp.float32))[0].astype(jnp.bfloat16)
        local_part = jnp.einsum('ncxyz,noxyz->co', values.astype(jnp.float32), pre_grad.astype(jnp.float32), precision=highest)
        mode_grad = forward_modes(pre_grad, forward_scaled)
        weight_part = weight_grads(spectra, mode_grad)
        input_modes = input_grads(weights, mode_grad)
        back_field = inverse_modes(input_modes, inverse_plain) + jnp.einsum('noxyz,co->ncxyz', pre_grad.astype(jnp.float32), local_f32, precision=highest)
        return ((running[0] + weight_part, running[1] + local_part), back_field[0].astype(jnp.bfloat16))
    start = (jnp.zeros((KX, KY * KZ, 2, C, CO), jnp.float32), jnp.zeros((C, CO), jnp.float32))
    (weight_sum, local_grad), grad_input = lax.scan(one_snapshot, start, (snapshots, cotangent))
    gradients = weight_sum.reshape(spectral_weight.shape)
    new_weight, new_first, new_second = adam_update(spectral_weight, first_moment, second_moment, gradients)
    return (grad_input, local_grad, new_weight, new_first, new_second)
```

```python
import math

import jax
import jax.numpy as jnp
import ml_dtypes
import numpy as np
from jax import lax
from jax.experimental import pallas as pl
from jax.experimental.pallas import tpu as pltpu
from jax.sharding import PartitionSpec as P

NX = 128
NY = 64
NZ = 128
KX = 32
KY = 32
KZ = 16
STEP = 100
C = 64
CO = 32
GRID = 64
DP = 4
RATE = 0.02

MESH = pl.DeviceIdType.MESH
F32 = jnp.float32
BF16 = jnp.bfloat16
NN = (((1,), (0,)), ((), ()))
NT = (((1,), (1,)), ((), ()))


def mode_numbers(length, retained):
    a = np.arange(retained)
    return np.where(a < retained // 2, a, length - retained + a)


def angles(length, numbers):
    points = np.arange(length)
    return (points[:, None] * numbers[None, :] % length) * (2.0 * math.pi / length)


def rotation(theta, direction):
    cos, sin = np.cos(theta), direction * np.sin(theta)
    return np.stack([np.stack([cos, sin]), np.stack([-sin, cos])])


def split_table(table):
    high = table.astype(ml_dtypes.bfloat16)
    low = (table - high.astype(np.float64)).astype(ml_dtypes.bfloat16)
    return np.stack([high, low])


def make_tables():
    z_angles = angles(NZ, np.arange(KZ))
    fold = np.where(np.arange(KZ) == 0, 1.0, 2.0) / (NX * NY * NZ)
    z_fwd = np.concatenate([np.cos(z_angles).T, -np.sin(z_angles).T]).astype(ml_dtypes.bfloat16)
    z_fwd_scaled = (z_fwd.astype(np.float64) * np.tile(fold, 2)[:, None]).astype(ml_dtypes.bfloat16)
    z_inv = np.concatenate([np.cos(z_angles).T, -np.sin(z_angles).T])
    z_inv_scaled = z_inv * np.tile(fold, 2)[:, None]

    def four(table):
        out = np.zeros((4, 2 * KZ, 4, NZ))
        for j in range(4):
            out[j, :, j] = table
        return split_table(out.reshape(4 * 2 * KZ, 4 * NZ))

    y_theta = angles(NY, mode_numbers(NY, KY))
    x_theta = angles(NX, mode_numbers(NX, KX))
    y_rot = rotation(y_theta, -1.0)
    x_rot = rotation(x_theta, -1.0)
    x_rot = x_rot.reshape(2, 2, GRID, 2, DP, KX // DP)
    yi_rot = rotation(y_theta.T, 1.0)
    xi_rot = rotation(x_theta.T, 1.0)
    xi_rot = xi_rot.reshape(2, 2, DP, KX // DP, GRID, 2)
    y_fwd = np.zeros((KY, 2, 2, 2, 2, 2, 2, NY))
    x_fwd = np.zeros((DP, 2, 2, 8, GRID, 2, 2, 2))
    x_inv = np.zeros((GRID, 2, 2, 2, DP, 2, 2, 8))
    y_inv = np.zeros((KY, 2, 2, 2, 2, 2, 2, NY))
    for c in range(2):
        x_fwd[:, c, :, :, :, c] = x_rot.transpose(4, 1, 5, 2, 3, 0)
        x_inv[:, c, :, :, :, c] = xi_rot.transpose(4, 5, 1, 2, 0, 3)
        for x in range(2):
            y_fwd[:, c, x, :, c, :, x] = y_rot.transpose(3, 1, 0, 2)
            y_inv[:, c, x, :, c, :, x] = yi_rot.transpose(2, 0, 1, 3)
    spread = np.zeros((8, 16, 8, 16, 32))
    for q in range(8):
        for c in range(16):
            spread[q, c, q, c] = 1.0
    gather = np.zeros((8, 4, 32, 32, 8))
    for q in range(8):
        for o in range(32):
            gather[q, :, o, o, q] = 1.0
    return (
        z_fwd,
        z_fwd_scaled,
        four(z_inv_scaled),
        four(z_inv),
        split_table(y_fwd.reshape(256, 512)),
        split_table(x_fwd.reshape(128, 512)),
        split_table(x_inv.reshape(512, 128)),
        split_table(y_inv.reshape(256, 512)),
        spread.reshape(8, 128, 512).astype(ml_dtypes.bfloat16),
        gather.reshape(1024, 256).astype(ml_dtypes.bfloat16),
    )


def dot(a, b, dims=NN):
    return lax.dot_general(a, b, dims, preferred_element_type=F32)


def split(a):
    high = a.astype(BF16)
    return high, (a - high.astype(F32)).astype(BF16)


def table_dot(table, values, dims=NN):
    high, low = split(values)
    return dot(table[0], high, dims) + dot(table[0], low, dims) + dot(table[1], high, dims)


def dot_table(values, table):
    high, low = split(values)
    return dot(high, table[0]) + dot(low, table[0]) + dot(high, table[1])


def dot_exact(values, table, dims=NN):
    high, low = split(values)
    return dot(high, table, dims) + dot(low, table, dims)


def kernel(
    snap, cot, lw, weight_hbm, first_hbm, second_hbm,
    z_fwd, z_fwd_scaled, z_inv_scaled, z_inv, y_fwd, x_fwd, x_inv, y_inv, spread, gather,
    out, local_out, new_weight_hbm, new_first_hbm, new_second_hbm,
    weight, first, second, new_weight, new_first, new_second,
    zb, snap_f, pre, back, grad_b, grad_f, ub, spec_x, mixed, grad_x,
    send1, recv1, send2, recv2, send3, recv3, send4, recv4,
    dsend1, drecv1, dsend2, drecv2, dsend3, drecv3, dsend4, drecv4,
    lsend, lrecv, send_sems, recv_sems, state_sems,
):
    d = lax.axis_index("dp")
    me = lax.axis_index("grid")
    slot_of = lambda g: (g % 2) * 32 + g // 2

    def load_state(i, _):
        lanes = pl.ds(pl.multiple_of(i * 128, 128), 128)
        for n, (src, dst) in enumerate(((weight_hbm, weight), (first_hbm, first), (second_hbm, second))):
            pltpu.make_async_copy(src.at[:, lanes], dst.at[i], state_sems.at[n]).start()
        return 0

    lax.fori_loop(0, 32, load_state, 0)

    barrier = pltpu.get_barrier_semaphore()

    def greet_grid(i, _):
        pl.semaphore_signal(barrier, inc=1, device_id={"grid": (me + i) % GRID}, device_id_type=MESH)
        return 0

    def greet_dp(i, _):
        pl.semaphore_signal(barrier, inc=1, device_id={"dp": (d + i) % DP}, device_id_type=MESH)
        return 0

    lax.fori_loop(1, GRID, greet_grid, 0)
    lax.fori_loop(1, DP, greet_dp, 0)

    def grid_send(n, src, dst, src_slot, dst_slot):
        def body(i, _):
            to = (me + i) % GRID
            pltpu.make_async_remote_copy(
                src_ref=src.at[src_slot(to)],
                dst_ref=dst.at[dst_slot(me)],
                send_sem=send_sems.at[n],
                recv_sem=recv_sems.at[n],
                device_id={"grid": to},
                device_id_type=MESH,
            ).start()
            return 0

        lax.fori_loop(1, GRID, body, 0)
        dst[dst_slot(me)] = src[src_slot(me)]

    def dp_send(n, src, dst):
        def body(i, _):
            to = (d + i) % DP
            pltpu.make_async_remote_copy(
                src_ref=src.at[to],
                dst_ref=dst.at[d],
                send_sem=send_sems.at[n],
                recv_sem=recv_sems.at[n],
                device_id={"dp": to},
                device_id_type=MESH,
            ).start()
            return 0

        lax.fori_loop(1, DP, body, 0)
        dst[d] = src[d]

    def wait_all(sems, n, ref):
        part = ref.at[pl.ds(0, ref.shape[0] - 1)]
        pltpu.make_async_copy(part, part, sems.at[n]).wait()

    place = lambda g: g

    def forward_zy(field, table, channels, send):
        half = channels // 2

        def body(i, _):
            values = field[pl.ds(i * 1024, 1024), :]
            z = dot(table[...], values, NT)
            c = i // (half // 8)
            row = (i % (half // 8)) * 64
            for r in range(2):
                for h in range(2):
                    for j in range(8):
                        zb[c * 2 + r, pl.ds(row + h * half * 8 + j * 8, 8), :] = z[
                            (r * 2 + h) * 8 : (r * 2 + h + 1) * 8, j * 128 : (j + 1) * 128
                        ]
            return 0

        lax.fori_loop(0, channels // 8, body, 0)
        rows = half * 8
        for h in range(2):
            values = jnp.concatenate([zb[j, h * rows : (h + 1) * rows, :] for j in range(4)], axis=1)
            result = table_dot(y_fwd, values, NT)
            send[h * 32 : (h + 1) * 32] = result.reshape(32, 8, rows)

    def forward_x(recv, send):
        lanes = recv.shape[2]
        result = table_dot(x_fwd, recv[...].reshape(512, lanes))
        send[...] = result.reshape(DP, 32, lanes)

    def inverse_x(recv, send):
        lanes = recv.shape[2]
        result = table_dot(x_inv, recv[...].reshape(128, lanes))
        send[...] = result.reshape(GRID, 8, lanes)

    def inverse_y(recv):
        lanes = recv.shape[2]
        for h in range(2):
            values = recv[h * 32 : (h + 1) * 32].reshape(256, lanes).T
            result = dot_table(values, y_inv)
            for j in range(4):
                ub[j, h * lanes : (h + 1) * lanes, :] = result[:, j * 128 : (j + 1) * 128]

    def inverse_z(table, channels, finish):
        lanes = channels * 4

        def body(i, _):
            c = i // (channels // 8)
            row = (i % (channels // 8)) * 32
            parts = [
                ub[c * 2 + s, pl.ds(row + h * lanes + j * 8, 8), :]
                for j in range(4) for s in range(2) for h in range(2)
            ]
            values = jnp.concatenate(parts, axis=0).T
            result = dot_table(values, table)
            for j in range(4):
                finish(pl.ds(i * 512 + j * 128, 128), result[:, j * 128 : (j + 1) * 128])
            return 0

        lax.fori_loop(0, channels // 4, body, 0)

    forward_zy(snap, z_fwd, C, send1)
    pl.semaphore_wait(barrier, GRID - 1 + DP - 1)
    grid_send(0, send1, recv1, slot_of, place)

    def widen(i, _):
        rows = pl.ds(i * 512, 512)
        snap_f[rows, :] = snap[rows, :].astype(F32)
        return 0

    lax.fori_loop(0, 16, widen, 0)
    lw_t = lw[...].astype(F32).T.astype(BF16)

    def strided(ref, cell, channels):
        return jnp.concatenate(
            [ref[pl.ds(cell * 4 + j, channels, stride=128), :] for j in range(4)], axis=1
        ).astype(BF16)

    def local_forward(i, _):
        result = dot(lw_t, strided(snap_f, i, C))
        for j in range(4):
            pre[pl.ds(i * 4 + j, CO, stride=128), :] = result[:, j * 128 : (j + 1) * 128]
        return 0

    lax.fori_loop(0, 32, local_forward, 0)
    wait_all(recv_sems, 0, recv1)

    forward_x(recv1, dsend1)
    dp_send(1, dsend1, drecv1)
    wait_all(recv_sems, 1, drecv1)

    spectra = drecv1[...].reshape(128, 256)
    spectra = jnp.concatenate([spectra[:, :128], spectra[:, 128:]], axis=0)
    spectra_high, spectra_low = split(spectra)

    def w_tiles(r, c, t):
        return range(r * 16 + c * 8 + t * 4, r * 16 + c * 8 + t * 4 + 4)

    def w_read(ref, q, r, c, t):
        return jnp.concatenate([ref[j, pl.ds(q, 8, stride=8), :] for j in w_tiles(r, c, t)], axis=1)

    def w_write(ref, q, r, c, t, value):
        for n, j in enumerate(w_tiles(r, c, t)):
            ref[j, pl.ds(q, 8, stride=8), :] = value[:, n * 128 : (n + 1) * 128]

    def s_rows(t, s, c, r):
        return pl.ds(((t * 4 + s) * 2 + c) * 16 + r * 8, 8)

    pltpu.make_async_copy(weight, weight, state_sems.at[0]).wait()

    def mix(q, _):
        spec_x[q] = dot(spectra_high, spread[q]) + dot(spectra_low, spread[q])
        sums = [[jnp.zeros((8, 128), F32) for _ in range(2)] for _ in range(4)]
        for c in range(2):
            for t in range(2):
                w_re = w_read(weight, q, 0, c, t)
                w_im = w_read(weight, q, 1, c, t)
                for s in range(4):
                    s_re = spec_x[q, s_rows(t, s, c, 0), :]
                    s_im = spec_x[q, s_rows(t, s, c, 1), :]
                    products = (s_re * w_re - s_im * w_im, s_re * w_im + s_im * w_re)
                    for r in range(2):
                        for j in range(4):
                            sums[s][r] = sums[s][r] + products[r][:, j * 128 : (j + 1) * 128]
        for s in range(4):
            for r in range(2):
                mixed[q, (s * 2 + r) * 8 : (s * 2 + r + 1) * 8, :] = sums[s][r]
        return 0

    lax.fori_loop(0, 8, mix, 0)
    values = jnp.concatenate([mixed[q] for q in range(8)], axis=1)
    result = dot_exact(values, gather[...])
    for c in range(2):
        dsend2[:, c * 16 : (c + 1) * 16, :] = result[:, c * 128 : (c + 1) * 128].reshape(4, 16, 128)
    dp_send(2, dsend2, drecv2)
    wait_all(recv_sems, 2, drecv2)

    inverse_x(drecv2, send2)
    grid_send(3, send2, recv2, place, slot_of)
    wait_all(recv_sems, 3, recv2)

    inverse_y(recv2)

    def through_gelu(rows, spectral):
        v = spectral + pre[rows, :]
        k = math.sqrt(2.0 / math.pi)
        square = v * v
        t = jnp.tanh(k * (v + 0.044715 * (square * v)))
        slope = 0.5 * (1.0 + t) + 0.5 * v * (1.0 - t * t) * (k * (1.0 + 3 * 0.044715 * square))
        value = (cot[rows, :].astype(F32) * slope).astype(BF16)
        grad_b[rows, :] = value
        grad_f[rows, :] = value.astype(F32)

    inverse_z(z_inv_scaled, CO, through_gelu)
    forward_zy(grad_b, z_fwd_scaled, CO, send3)
    grid_send(4, send3, recv3, slot_of, place)

    lsend[...] = jnp.zeros_like(lsend)

    def local_backward(i, total):
        g = strided(grad_f, i, CO)
        result = dot(lw[...], g)
        for j in range(4):
            back[pl.ds(i * 4 + j, C, stride=128), :] = result[:, j * 128 : (j + 1) * 128]
        return total + dot(g, strided(snap_f, i, C), NT)

    total = lax.fori_loop(0, 32, local_backward, jnp.zeros((CO, C), F32))
    gx, gz, gy = me // 16, me // 4 % 4, me % 4
    rounds = (
        (gy, lambda j: {"grid": me - gy + j}),
        (gz, lambda j: {"grid": me - 4 * gz + 4 * j}),
        (gx, lambda j: {"grid": me - 16 * gx + 16 * j}),
        (d, lambda j: {"dp": j}),
    )

    def local_send(n, value):
        mine, device = rounds[n]
        lsend[n, :, 0:C] = value

        def body(i, _):
            pltpu.make_async_remote_copy(
                src_ref=lsend.at[n],
                dst_ref=lrecv.at[n, mine],
                send_sem=send_sems.at[8 + n],
                recv_sem=recv_sems.at[8 + n],
                device_id=device((mine + i) % 4),
                device_id_type=MESH,
            ).start()
            return 0

        lax.fori_loop(1, 4, body, 0)
        lrecv[n, mine] = lsend[n]

    def local_sum(n):
        wait_all(recv_sems, 8 + n, lrecv.at[n])
        return ((lrecv[n, 0] + lrecv[n, 1]) + (lrecv[n, 2] + lrecv[n, 3]))[:, 0:C]

    local_send(0, total)
    wait_all(recv_sems, 4, recv3)

    forward_x(recv3, dsend3)
    dp_send(5, dsend3, drecv3)
    local_send(1, local_sum(0))
    wait_all(recv_sems, 5, drecv3)

    values = jnp.concatenate(
        [drecv3[:, c * 16 : (c + 1) * 16, :].reshape(64, 128) for c in range(2)], axis=1
    )
    result = dot_exact(values, gather[...], NT)
    for q in range(8):
        grad_x[q] = result[:, q * 128 : (q + 1) * 128]

    def g_tile(q, s, r):
        tile = grad_x[q, (s * 2 + r) * 8 : (s * 2 + r + 1) * 8, :]
        return jnp.concatenate([tile] * 4, axis=1)

    def input_modes(q, total):
        parts = {}
        for c in range(2):
            for t in range(2):
                w_re = w_read(weight, q, 0, c, t)
                w_im = w_read(weight, q, 1, c, t)
                for s in range(4):
                    g_re, g_im = g_tile(q, s, 0), g_tile(q, s, 1)
                    parts[t, s, c, 0] = w_re * g_re + w_im * g_im
                    parts[t, s, c, 1] = w_re * g_im - w_im * g_re
        values = jnp.concatenate(
            [parts[t, s, c, r] for t in range(2) for s in range(4) for c in range(2) for r in range(2)],
            axis=0,
        )
        return total + dot_exact(values, spread[q], NT)

    total = lax.fori_loop(0, 8, input_modes, jnp.zeros((256, 128), F32))
    for t in range(2):
        dsend4[:, :, t * 128 : (t + 1) * 128] = total[t * 128 : (t + 1) * 128].reshape(4, 32, 128)
    dp_send(6, dsend4, drecv4)
    local_send(2, local_sum(1))
    wait_all(recv_sems, 6, drecv4)

    inverse_x(drecv4, send4)
    grid_send(7, send4, recv4, place, slot_of)
    local_send(3, local_sum(2))

    pltpu.make_async_copy(first, first, state_sems.at[1]).wait()
    pltpu.make_async_copy(second, second, state_sems.at[2]).wait()

    def adam(q, _):
        for c in range(2):
            for t in range(2):
                re = im = None
                for s in range(4):
                    s_re = spec_x[q, s_rows(t, s, c, 0), :]
                    s_im = spec_x[q, s_rows(t, s, c, 1), :]
                    g_re, g_im = g_tile(q, s, 0), g_tile(q, s, 1)
                    a, b = s_re * g_re + s_im * g_im, s_re * g_im - s_im * g_re
                    re, im = (a, b) if re is None else (re + a, im + b)
                for r, g in enumerate((re, im)):
                    m = 0.9 * w_read(first, q, r, c, t) + 0.1 * g
                    v = 0.999 * w_read(second, q, r, c, t) + 0.001 * g * g
                    step = (m / (1.0 - 0.9**STEP)) / (jnp.sqrt(v / (1.0 - 0.999**STEP)) + 1e-8)
                    w_write(new_first, q, r, c, t, m)
                    w_write(new_second, q, r, c, t, v)
                    w_write(new_weight, q, r, c, t, w_read(weight, q, r, c, t) - RATE * step)
        return 0

    lax.fori_loop(0, 8, adam, 0)
    states = ((new_weight, new_weight_hbm), (new_first, new_first_hbm), (new_second, new_second_hbm))

    def store_state(i, _):
        lanes = pl.ds(pl.multiple_of(i * 128, 128), 128)
        for n, (src, dst) in enumerate(states):
            pltpu.make_async_copy(src.at[i], dst.at[:, lanes], state_sems.at[3 + n]).start()
        return 0

    lax.fori_loop(0, 32, store_state, 0)
    local_out[...] = local_sum(3).T
    wait_all(recv_sems, 7, recv4)

    inverse_y(recv4)

    def finish(rows, spectral):
        out[rows, :] = (spectral + back[rows, :]).astype(BF16)

    inverse_z(z_inv, C, finish)

    for n, ref in enumerate((send1, dsend1, dsend2, send2, send3, dsend3, dsend4, send4)):
        wait_all(send_sems, n, ref)
    for n in range(4):
        wait_all(send_sems, 8 + n, lrecv.at[n])
    for n, (src, _) in enumerate(states):
        pltpu.make_async_copy(src, src, state_sems.at[3 + n]).wait()


def on_device(tables, snapshots, cotangent, local_weight, spectral_weight, first_moment, second_moment):
    vmem = pl.BlockSpec(memory_space=pltpu.VMEM)
    hbm = pl.BlockSpec(memory_space=pl.ANY)
    shape = jax.ShapeDtypeStruct
    state = shape((64, 4096), F32)
    big, small = (GRID, 8, 256), (GRID, 8, 128)
    dbig, dsmall = (DP, 32, 256), (DP, 32, 128)
    results = pl.pallas_call(
        kernel,
        out_shape=(shape((8192, 128), BF16), shape((C, CO), F32), state, state, state),
        in_specs=[vmem] * 3 + [hbm] * 3 + [vmem] * len(tables),
        out_specs=(vmem,) * 2 + (hbm,) * 3,
        scratch_shapes=[pltpu.VMEM((32, 64, 128), F32)] * 6
        + [
            pltpu.VMEM((4, 512, 128), F32),
            pltpu.VMEM((8192, 128), F32),
            pltpu.VMEM((4096, 128), F32),
            pltpu.VMEM((8192, 128), F32),
            pltpu.VMEM((4096, 128), BF16),
            pltpu.VMEM((4096, 128), F32),
            pltpu.VMEM((4, 512, 128), F32),
            pltpu.VMEM((8, 256, 512), F32),
            pltpu.VMEM((8, 64, 128), F32),
            pltpu.VMEM((8, 64, 128), F32),
        ]
        + [pltpu.VMEM(s, F32) for s in (big, big, small, small, small, small, big, big)]
        + [pltpu.VMEM(s, F32) for s in (dbig, dbig, dsmall, dsmall, dsmall, dsmall, dbig, dbig)]
        + [
            pltpu.VMEM((4, CO, 128), F32),
            pltpu.VMEM((4, 4, CO, 128), F32),
            pltpu.SemaphoreType.DMA((12,)),
            pltpu.SemaphoreType.DMA((12,)),
            pltpu.SemaphoreType.DMA((6,)),
        ],
        compiler_params=pltpu.CompilerParams(
            collective_id=0, has_side_effects=True, vmem_limit_bytes=56 * 1024 * 1024
        ),
    )(
        snapshots.reshape(8192, 128),
        cotangent.reshape(4096, 128),
        local_weight,
        spectral_weight.reshape(64, 4096),
        first_moment.reshape(64, 4096),
        second_moment.reshape(64, 4096),
        *tables,
    )
    grad_input, local_grad, new_weight, new_first, new_second = results
    return (
        grad_input.reshape(snapshots.shape),
        local_grad,
        new_weight.reshape(spectral_weight.shape),
        new_first.reshape(spectral_weight.shape),
        new_second.reshape(spectral_weight.shape),
    )


def solution(mesh):
    tables = make_tables()
    split_spec = P("dp", "grid", None)
    field_spec = P("dp", None, "grid", None, None)

    def step(*args):
        return on_device(tables, *args)

    return jax.shard_map(
        step,
        mesh=mesh,
        in_specs=(field_spec, field_spec, P(), split_spec, split_spec, split_spec),
        out_specs=(field_spec, P(), split_spec, split_spec, split_spec),
        check_vma=False,
    )
```

```python
import math

import jax
import jax.numpy as jnp
import ml_dtypes
import numpy as np
from jax import lax
from jax.experimental import pallas as pl
from jax.experimental.pallas import tpu as pltpu
from jax.sharding import PartitionSpec as P

NX = 128
NY = 64
NZ = 128
KX = 32
KY = 32
KZ = 16
STEP = 100
C = 64
CO = 32
GRID = 64
DP = 4
RATE = 0.02

MESH = pl.DeviceIdType.MESH
F32 = jnp.float32
BF16 = jnp.bfloat16
NN = (((1,), (0,)), ((), ()))
NT = (((1,), (1,)), ((), ()))


def mode_numbers(length, retained):
    a = np.arange(retained)
    return np.where(a < retained // 2, a, length - retained + a)


def angles(length, numbers):
    points = np.arange(length)
    return (points[:, None] * numbers[None, :] % length) * (2.0 * math.pi / length)


def rotation(theta, direction):
    cos, sin = np.cos(theta), direction * np.sin(theta)
    return np.stack([np.stack([cos, sin]), np.stack([-sin, cos])])


def split_table(table):
    high = table.astype(ml_dtypes.bfloat16)
    low = (table - high.astype(np.float64)).astype(ml_dtypes.bfloat16)
    return np.stack([high, low])


def make_tables():
    z_angles = angles(NZ, np.arange(KZ))
    fold = np.where(np.arange(KZ) == 0, 1.0, 2.0) / (NX * NY * NZ)
    z_fwd = np.concatenate([np.cos(z_angles).T, -np.sin(z_angles).T]).astype(ml_dtypes.bfloat16)
    z_fwd_scaled = (z_fwd.astype(np.float64) * np.tile(fold, 2)[:, None]).astype(ml_dtypes.bfloat16)
    z_inv = np.concatenate([np.cos(z_angles).T, -np.sin(z_angles).T])
    z_inv_scaled = z_inv * np.tile(fold, 2)[:, None]

    def four(table):
        out = np.zeros((4, 2 * KZ, 4, NZ))
        for j in range(4):
            out[j, :, j] = table
        return split_table(out.reshape(4 * 2 * KZ, 4 * NZ))

    y_theta = angles(NY, mode_numbers(NY, KY))
    x_theta = angles(NX, mode_numbers(NX, KX))
    y_rot = rotation(y_theta, -1.0)
    x_rot = rotation(x_theta, -1.0)
    x_rot = x_rot.reshape(2, 2, GRID, 2, DP, KX // DP)
    yi_rot = rotation(y_theta.T, 1.0)
    xi_rot = rotation(x_theta.T, 1.0)
    xi_rot = xi_rot.reshape(2, 2, DP, KX // DP, GRID, 2)
    y_fwd = np.zeros((KY, 2, 2, 2, 2, 2, 2, NY))
    x_fwd = np.zeros((DP, 2, 2, 8, GRID, 2, 2, 2))
    x_inv = np.zeros((GRID, 2, 2, 2, DP, 2, 2, 8))
    y_inv = np.zeros((KY, 2, 2, 2, 2, 2, 2, NY))
    for c in range(2):
        x_fwd[:, c, :, :, :, c] = x_rot.transpose(4, 1, 5, 2, 3, 0)
        x_inv[:, c, :, :, :, c] = xi_rot.transpose(4, 5, 1, 2, 0, 3)
        for x in range(2):
            y_fwd[:, c, x, :, c, :, x] = y_rot.transpose(3, 1, 0, 2)
            y_inv[:, c, x, :, c, :, x] = yi_rot.transpose(2, 0, 1, 3)
    spread = np.zeros((8, 16, 8, 16, 32))
    for q in range(8):
        for c in range(16):
            spread[q, c, q, c] = 1.0
    gather = np.zeros((8, 4, 32, 32, 8))
    for q in range(8):
        for o in range(32):
            gather[q, :, o, o, q] = 1.0
    return (
        z_fwd,
        z_fwd_scaled,
        four(z_inv_scaled),
        four(z_inv),
        split_table(y_fwd.reshape(256, 512)),
        split_table(x_fwd.reshape(128, 512)),
        split_table(x_inv.reshape(512, 128)),
        split_table(y_inv.reshape(256, 512)),
        spread.reshape(8, 128, 512).astype(ml_dtypes.bfloat16),
        gather.reshape(1024, 256).astype(ml_dtypes.bfloat16),
    )


def dot(a, b, dims=NN):
    return lax.dot_general(a, b, dims, preferred_element_type=F32)


def split(a):
    high = a.astype(BF16)
    return high, (a - high.astype(F32)).astype(BF16)


def table_dot(table, values, dims=NN):
    high, low = split(values)
    return dot(table[0], high, dims) + dot(table[0], low, dims) + dot(table[1], high, dims)


def dot_table(values, table):
    high, low = split(values)
    return dot(high, table[0]) + dot(low, table[0]) + dot(high, table[1])


def dot_exact(values, table, dims=NN):
    high, low = split(values)
    return dot(high, table, dims) + dot(low, table, dims)


def dp_and_grid():
    return lax.axis_index("dp"), lax.axis_index("grid")


def inverse_y(recv, table, ub):
    for h in range(2):
        values = recv[h * 32 : (h + 1) * 32].reshape(256, 128).T
        result = dot_table(values, table)
        for j in range(4):
            ub[j, h * 128 : (h + 1) * 128, :] = result[:, j * 128 : (j + 1) * 128]


def inverse_z(ub, table, finish):
    def body(i, _):
        c = lax.div(i, 4)
        row = lax.rem(i, 4) * 32
        parts = [
            ub[c * 2 + s, pl.ds(row + h * 128 + j * 8, 8), :]
            for j in range(4) for s in range(2) for h in range(2)
        ]
        values = jnp.concatenate(parts, axis=0).T
        result = dot_table(values, table)
        for j in range(4):
            finish(pl.ds(i * 512 + j * 128, 128), result[:, j * 128 : (j + 1) * 128])
        return 0

    lax.fori_loop(0, 8, body, 0)


TABLES = (
    "z_fwd", "z_fwd_scaled", "z_inv_scaled", "z_inv", "y_fwd", "x_fwd", "x_inv", "y_inv", "spread", "gather"
)


def kernel(
    snap_hbm, cot_hbm, lw_hbm, weight_hbm, first_hbm, second_hbm,
    z_fwd_hbm, z_fwd_scaled_hbm, z_inv_scaled_hbm, z_inv_hbm, y_fwd_hbm, x_fwd_hbm, x_inv_hbm, y_inv_hbm,
    spread_hbm, gather_hbm,
    last_hbm, back_hbm, half_hbm, local_out, new_weight_hbm, new_first_hbm, new_second_hbm,
    snap, cot, lw_t, z_fwd, z_fwd_scaled, z_inv_scaled, z_inv, y_fwd, x_fwd, x_inv, y_inv, spread, gather,
    weight, first, second, new_weight, new_first, new_second,
    zb, snap_f, pre, back_a, back_b, grad_b, grad_f, ub, spec_x, mixed, grad_x, half,
    gsend, grecv, dsend, drecv, lsend, lrecv,
    load_sems, state_sems, out_sems, gsend_sems, grecv_sems, dsend_sems, drecv_sems, lsend_sems, lrecv_sems,
):
    d, me = dp_and_grid()
    slot_of = lambda g: lax.rem(g, 2) * 32 + lax.div(g, 2)
    place = lambda g: g
    pending, stored = [], []

    loads = {}

    def load(name, src, dst):
        copy = pltpu.make_async_copy(src, dst, load_sems.at[len(loads)])
        copy.start()
        loads[name] = copy

    def need(*names):
        for name in names:
            loads.pop(name).wait()

    def snap_rows(t, c):
        return pl.ds(c * 4096 + t * 2048, 2048)

    def load_snap(t, c, n):
        rows = snap_rows(t, c)
        return pltpu.make_async_copy(snap_hbm.at[rows], snap.at[rows], state_sems.at[n])

    load("z_fwd", z_fwd_hbm, z_fwd)
    load_snap(0, 0, 6).start()
    load_snap(0, 1, 7).start()
    load("y_fwd", y_fwd_hbm, y_fwd)
    load_snap(1, 0, 8).start()
    load_snap(1, 1, 9).start()

    barrier = pltpu.get_barrier_semaphore()

    def greet_grid(i, _):
        pl.semaphore_signal(barrier, inc=1, device_id={"grid": lax.rem(me + i, GRID)}, device_id_type=MESH)
        return 0

    def greet_dp(i, _):
        pl.semaphore_signal(barrier, inc=1, device_id={"dp": lax.rem(d + i, DP)}, device_id_type=MESH)
        return 0

    lax.fori_loop(1, GRID, greet_grid, 0)
    lax.fori_loop(1, DP, greet_dp, 0)

    load("x_fwd", x_fwd_hbm, x_fwd)
    load("spread", spread_hbm, spread)

    def load_state(n, src, dst):
        def body(i, _):
            lanes = pl.ds(pl.multiple_of(i * 128, 128), 128)
            pltpu.make_async_copy(src.at[:, lanes], dst.at[i], state_sems.at[n]).start()
            return 0

        lax.fori_loop(0, 32, body, 0)

    def need_state(n, dst):
        pltpu.make_async_copy(dst, dst, state_sems.at[n]).wait()

    load_state(0, weight_hbm, weight)
    load("gather", gather_hbm, gather)
    load("lw", lw_hbm, lw_t)
    load("x_inv", x_inv_hbm, x_inv)
    load("y_inv", y_inv_hbm, y_inv)
    load("z_inv_scaled", z_inv_scaled_hbm, z_inv_scaled)
    load("cot", cot_hbm, cot)
    load("z_fwd_scaled", z_fwd_scaled_hbm, z_fwd_scaled)
    load_state(1, first_hbm, first)
    load_state(2, second_hbm, second)
    load("z_inv", z_inv_hbm, z_inv)

    def grid_send(n, src_slot, dst_slot):
        def body(i, _):
            to = lax.rem(me + i, GRID)
            pltpu.make_async_remote_copy(
                src_ref=gsend.at[n, src_slot(to)],
                dst_ref=grecv.at[n, dst_slot(me)],
                send_sem=gsend_sems.at[n],
                recv_sem=grecv_sems.at[n],
                device_id={"grid": to},
                device_id_type=MESH,
            ).start()
            return 0

        lax.fori_loop(1, GRID, body, 0)
        grecv[n, dst_slot(me)] = gsend[n, src_slot(me)]
        pending.append((gsend_sems, n, gsend.at[n]))

    def dp_send(n):
        def body(i, _):
            to = lax.rem(d + i, DP)
            pltpu.make_async_remote_copy(
                src_ref=dsend.at[n, to],
                dst_ref=drecv.at[n, d],
                send_sem=dsend_sems.at[n],
                recv_sem=drecv_sems.at[n],
                device_id={"dp": to},
                device_id_type=MESH,
            ).start()
            return 0

        lax.fori_loop(1, DP, body, 0)
        drecv[n, d] = dsend[n, d]
        pending.append((dsend_sems, n, dsend.at[n]))

    def wait_all(sems, n, ref):
        part = ref.at[pl.ds(0, ref.shape[0] - 1)]
        pltpu.make_async_copy(part, part, sems.at[n]).wait()

    def grid_wait(n):
        wait_all(grecv_sems, n, grecv.at[n])

    def dp_wait(n):
        wait_all(drecv_sems, n, drecv.at[n])

    def forward_z(field, row_of, table, c):
        for part in range(2):
            start = row_of(c) + part * 1024
            z = dot(table[...], field[pl.ds(start, 1024), :], NT)
            for r in range(2):
                for h in range(2):
                    for j in range(8):
                        row = h * 128 + (part * 8 + j) * 8
                        zb[c * 2 + r, row : row + 8, :] = z[
                            (r * 2 + h) * 8 : (r * 2 + h + 1) * 8, j * 128 : (j + 1) * 128
                        ]

    def forward_y(n):
        for h in range(2):
            values = jnp.concatenate([zb[j, h * 128 : (h + 1) * 128, :] for j in range(4)], axis=1)
            result = table_dot(y_fwd, values, NT)
            gsend[n, h * 32 : (h + 1) * 32] = result.reshape(32, 8, 128)

    def forward_x(n, m):
        result = table_dot(x_fwd, grecv[n].reshape(512, 128))
        dsend[m] = result.reshape(DP, 32, 128)

    def inverse_x(m, n):
        result = table_dot(x_inv, drecv[m].reshape(128, 128))
        gsend[n] = result.reshape(GRID, 8, 128)

    need("z_fwd")
    for t in range(2):
        for c in range(2):
            load_snap(t, c, 6 + t * 2 + c).wait()
            forward_z(snap, lambda c: c * 4096 + t * 2048, z_fwd, c)
        if t == 0:
            need("y_fwd")
        forward_y(t)
        if t == 0:
            pl.semaphore_wait(barrier, GRID - 1 + DP - 1)
        grid_send(t, slot_of, place)

    def widen(i, _):
        rows = pl.ds(i * 512, 512)
        snap_f[rows, :] = snap[rows, :].astype(F32)
        return 0

    lax.fori_loop(0, 16, widen, 0)

    need("x_fwd")
    for t in range(2):
        grid_wait(t)
        forward_x(t, t)
        dp_send(t)

    def w_tiles(r, c, t):
        return range(r * 16 + c * 8 + t * 4, r * 16 + c * 8 + t * 4 + 4)

    def w_read(ref, q, r, c, t):
        return jnp.concatenate([ref[j, pl.ds(q, 8, stride=8), :] for j in w_tiles(r, c, t)], axis=1)

    def w_write(ref, q, r, c, t, value):
        for n, j in enumerate(w_tiles(r, c, t)):
            ref[j, pl.ds(q, 8, stride=8), :] = value[:, n * 128 : (n + 1) * 128]

    def s_rows(t, s, c, r):
        return pl.ds(((t * 4 + s) * 2 + c) * 16 + r * 8, 8)

    def mix(t):
        high, low = split(drecv[t].reshape(128, 128))

        def body(q, _):
            spec_x[q, t * 128 : (t + 1) * 128] = dot(high, spread[q]) + dot(low, spread[q])
            if t == 0:
                sums = [[jnp.zeros((8, 128), F32) for _ in range(2)] for _ in range(4)]
            else:
                sums = [[mixed[q, (s * 2 + r) * 8 : (s * 2 + r + 1) * 8, :] for r in range(2)] for s in range(4)]
            for c in range(2):
                w_re, w_im = w_read(weight, q, 0, c, t), w_read(weight, q, 1, c, t)
                for s in range(4):
                    s_re = spec_x[q, s_rows(t, s, c, 0), :]
                    s_im = spec_x[q, s_rows(t, s, c, 1), :]
                    products = (s_re * w_re - s_im * w_im, s_re * w_im + s_im * w_re)
                    for r in range(2):
                        for j in range(4):
                            sums[s][r] = sums[s][r] + products[r][:, j * 128 : (j + 1) * 128]
            for s in range(4):
                for r in range(2):
                    mixed[q, (s * 2 + r) * 8 : (s * 2 + r + 1) * 8, :] = sums[s][r]
            return 0

        lax.fori_loop(0, 8, body, 0)

    need("spread")
    need_state(0, weight)
    for t in range(2):
        dp_wait(t)
        mix(t)
    need("gather")
    values = jnp.concatenate([mixed[q] for q in range(8)], axis=1)
    result = dot_exact(values, gather[...])
    for c in range(2):
        dsend[2, :, c * 16 : (c + 1) * 16, :] = result[:, c * 128 : (c + 1) * 128].reshape(4, 16, 128)
    dp_send(2)
    need("x_inv")
    dp_wait(2)

    inverse_x(2, 2)
    grid_send(2, place, slot_of)

    def strided(ref, cell, channels):
        return jnp.concatenate(
            [ref[pl.ds(cell * 4 + j, channels, stride=128), :] for j in range(4)], axis=1
        ).astype(BF16)

    def local_forward(i, _):
        result = dot(lw_t[...], strided(snap_f, i, C))
        for j in range(4):
            pre[pl.ds(i * 4 + j, CO, stride=128), :] = result[:, j * 128 : (j + 1) * 128]
        return 0

    need("lw")
    lax.fori_loop(0, 32, local_forward, 0)
    lw = lw_t[...].astype(F32).T.astype(BF16)
    need("y_inv", "z_inv_scaled", "cot")
    grid_wait(2)

    inverse_y(grecv.at[2], y_inv, ub)

    def through_gelu(rows, spectral):
        v = spectral + pre[rows, :]
        k = math.sqrt(2.0 / math.pi)
        square = v * v
        t = jnp.tanh(k * (v + 0.044715 * (square * v)))
        slope = 0.5 * (1.0 + t) + 0.5 * v * (1.0 - t * t) * (k * (1.0 + 3 * 0.044715 * square))
        value = (cot[rows, :].astype(F32) * slope).astype(BF16)
        grad_b[rows, :] = value
        grad_f[rows, :] = value.astype(F32)

    inverse_z(ub, z_inv_scaled, through_gelu)
    need("z_fwd_scaled")
    for c in range(2):
        forward_z(grad_b, lambda c: c * 2048, z_fwd_scaled, c)
    forward_y(3)
    grid_send(3, slot_of, place)

    lsend[...] = jnp.zeros_like(lsend)

    def local_grad(i, total):
        return total + dot(strided(grad_f, i, CO), strided(snap_f, i, C), NT)

    total = lax.fori_loop(0, 32, local_grad, jnp.zeros((CO, C), F32))
    gx, gz, gy = lax.div(me, 16), lax.rem(lax.div(me, 4), 4), lax.rem(me, 4)
    rounds = (
        (gy, lambda j: {"grid": me - gy + j}),
        (gz, lambda j: {"grid": me - 4 * gz + 4 * j}),
        (gx, lambda j: {"grid": me - 16 * gx + 16 * j}),
        (d, lambda j: {"dp": j}),
    )

    def local_send(n, value):
        mine, device = rounds[n]
        lsend[n, :, 0:C] = value

        def body(i, _):
            pltpu.make_async_remote_copy(
                src_ref=lsend.at[n],
                dst_ref=lrecv.at[n, mine],
                send_sem=lsend_sems.at[n],
                recv_sem=lrecv_sems.at[n],
                device_id=device(lax.rem(mine + i, 4)),
                device_id_type=MESH,
            ).start()
            return 0

        lax.fori_loop(1, 4, body, 0)
        lrecv[n, mine] = lsend[n]
        pending.append((lsend_sems, n, lrecv.at[n]))

    def local_sum(n):
        wait_all(lrecv_sems, n, lrecv.at[n])
        return ((lrecv[n, 0] + lrecv[n, 1]) + (lrecv[n, 2] + lrecv[n, 3]))[:, 0:C]

    local_send(0, total)
    grid_wait(3)

    forward_x(3, 3)
    dp_send(3)
    dp_wait(3)

    values = jnp.concatenate(
        [drecv[3, :, c * 16 : (c + 1) * 16, :].reshape(64, 128) for c in range(2)], axis=1
    )
    result = dot_exact(values, gather[...], NT)
    for q in range(8):
        grad_x[q] = result[:, q * 128 : (q + 1) * 128]

    def g_tile(q, s, r):
        tile = grad_x[q, (s * 2 + r) * 8 : (s * 2 + r + 1) * 8, :]
        return jnp.concatenate([tile] * 4, axis=1)

    def input_modes(t):
        def body(q, total):
            parts = {}
            for c in range(2):
                w_re, w_im = w_read(weight, q, 0, c, t), w_read(weight, q, 1, c, t)
                for s in range(4):
                    g_re, g_im = g_tile(q, s, 0), g_tile(q, s, 1)
                    parts[s, c, 0] = w_re * g_re + w_im * g_im
                    parts[s, c, 1] = w_re * g_im - w_im * g_re
            values = jnp.concatenate(
                [parts[s, c, r] for s in range(4) for c in range(2) for r in range(2)], axis=0
            )
            return total + dot_exact(values, spread[q], NT)

        total = lax.fori_loop(0, 8, body, jnp.zeros((128, 128), F32))
        dsend[4 + t] = total.reshape(4, 32, 128)

    for t in range(2):
        input_modes(t)
        dp_send(4 + t)
    local_send(1, local_sum(0))

    need_state(1, first)
    need_state(2, second)

    def adam(q, _):
        for c in range(2):
            for t in range(2):
                re = im = None
                for s in range(4):
                    s_re = spec_x[q, s_rows(t, s, c, 0), :]
                    s_im = spec_x[q, s_rows(t, s, c, 1), :]
                    g_re, g_im = g_tile(q, s, 0), g_tile(q, s, 1)
                    a, b = s_re * g_re + s_im * g_im, s_re * g_im - s_im * g_re
                    re, im = (a, b) if re is None else (re + a, im + b)
                for r, g in enumerate((re, im)):
                    m = 0.9 * w_read(first, q, r, c, t) + 0.1 * g
                    v = 0.999 * w_read(second, q, r, c, t) + 0.001 * g * g
                    step = (m / (1.0 - 0.9**STEP)) / (jnp.sqrt(v / (1.0 - 0.999**STEP)) + 1e-8)
                    w_write(new_first, q, r, c, t, m)
                    w_write(new_second, q, r, c, t, v)
                    w_write(new_weight, q, r, c, t, w_read(weight, q, r, c, t) - RATE * step)
        return 0

    lax.fori_loop(0, 4, adam, 0)
    for t in range(2):
        dp_wait(4 + t)
        inverse_x(4 + t, 4 + t)
        grid_send(4 + t, place, slot_of)
    local_send(2, local_sum(1))

    def local_backward(i, _):
        result = dot(lw, strided(grad_f, i, CO))
        for j in range(4):
            for c in range(2):
                for t, ref in enumerate((back_a, back_b)):
                    row = c * 32 + t * 16
                    ref[pl.ds(c * 2048 + i * 4 + j, 16, stride=128), :] = result[
                        row : row + 16, j * 128 : (j + 1) * 128
                    ]
        return 0

    def store(n, src, dst):
        copy = pltpu.make_async_copy(src, dst, out_sems.at[n])
        copy.start()
        stored.append(copy)

    lax.fori_loop(0, 32, local_backward, 0)
    store(0, back_b, back_hbm)
    local_send(3, local_sum(2))
    lax.fori_loop(4, 8, adam, 0)
    states = ((new_weight, new_weight_hbm), (new_first, new_first_hbm), (new_second, new_second_hbm))

    def store_state(i, _):
        lanes = pl.ds(pl.multiple_of(i * 128, 128), 128)
        for n, (src, dst) in enumerate(states):
            pltpu.make_async_copy(src.at[i], dst.at[:, lanes], state_sems.at[3 + n]).start()
        return 0

    lax.fori_loop(0, 32, store_state, 0)
    need("z_inv")
    grid_wait(4)
    inverse_y(grecv.at[4], y_inv, ub)

    def finish(rows, spectral):
        half[rows, :] = (spectral + back_a[rows, :]).astype(BF16)

    inverse_z(ub, z_inv, finish)
    store(1, half, half_hbm)
    local_out[...] = local_sum(3)
    grid_wait(5)
    store(2, grecv.at[5], last_hbm)

    for sems, n, ref in pending:
        wait_all(sems, n, ref)
    for n, (src, _) in enumerate(states):
        need_state(3 + n, src)
    for copy in stored:
        copy.wait()


def last_kernel(
    last, back_hbm, half_hbm, local, weight_hbm, first_hbm, second_hbm, y_inv, z_inv,
    out_hbm, local_out, new_weight_hbm, new_first_hbm, new_second_hbm,
    back, ub, half, half_a, weight, first, second, in_sems, out_sems,
):
    back_copy = pltpu.make_async_copy(back_hbm, back, in_sems.at[0])
    back_copy.start()
    ways = (
        (half_hbm, half_a, None),
        (weight_hbm, weight, new_weight_hbm),
        (first_hbm, first, new_first_hbm),
        (second_hbm, second, new_second_hbm),
    )
    copies = [pltpu.make_async_copy(src, via, in_sems.at[1 + n]) for n, (src, via, _) in enumerate(ways)]
    for copy in copies:
        copy.start()

    def half_out(t, src):
        return [
            pltpu.make_async_copy(
                src.at[pl.ds(c * 2048, 2048)],
                out_hbm.at[pl.ds(c * 4096 + t * 2048, 2048)],
                out_sems.at[t * 2 + c],
            )
            for c in range(2)
        ]

    local_out[...] = local[...]
    inverse_y(last, y_inv, ub)
    stores = []
    for n, (copy, (_, via, dst)) in enumerate(zip(copies, ways)):
        copy.wait()
        for out in half_out(0, via) if dst is None else [pltpu.make_async_copy(via, dst, out_sems.at[3 + n])]:
            out.start()
            stores.append(out)
    back_copy.wait()

    def finish(rows, spectral):
        half[rows, :] = (spectral + back[rows, :]).astype(BF16)

    inverse_z(ub, z_inv, finish)
    for out in half_out(1, half):
        out.start()
        stores.append(out)
    for out in stores:
        out.wait()


def on_device(tables, snapshots, cotangent, local_weight, spectral_weight, first_moment, second_moment):
    vmem = pl.BlockSpec(memory_space=pltpu.VMEM)
    hbm = pl.BlockSpec(memory_space=pl.ANY)
    shape = jax.ShapeDtypeStruct
    state = shape((64, 4096), F32)
    state_scratch = pltpu.VMEM((32, 64, 128), F32)
    sems = lambda n: pltpu.SemaphoreType.DMA((n,))
    table_scratch = [pltpu.VMEM(table.shape, BF16) for table in tables]
    params = lambda **more: pltpu.CompilerParams(
        has_side_effects=True, vmem_limit_bytes=56 * 1024 * 1024, **more
    )
    last, back, half, local_grad, new_weight, new_first, new_second = pl.pallas_call(
        kernel,
        out_shape=(
            shape((GRID, 8, 128), F32), shape((4096, 128), F32), shape((4096, 128), BF16), shape((CO, C), F32),
            state, state, state,
        ),
        in_specs=[hbm] * (6 + len(tables)),
        out_specs=(hbm,) * 3 + (vmem,) + (hbm,) * 3,
        scratch_shapes=[
            pltpu.VMEM((8192, 128), BF16),
            pltpu.VMEM((4096, 128), BF16),
            pltpu.VMEM((CO, C), BF16),
        ]
        + table_scratch
        + [state_scratch] * 6
        + [
            pltpu.VMEM((4, 256, 128), F32),
            pltpu.VMEM((8192, 128), F32),
            pltpu.VMEM((4096, 128), F32),
            pltpu.VMEM((4096, 128), F32),
            pltpu.VMEM((4096, 128), F32),
            pltpu.VMEM((4096, 128), BF16),
            pltpu.VMEM((4096, 128), F32),
            pltpu.VMEM((4, 256, 128), F32),
            pltpu.VMEM((8, 256, 512), F32),
            pltpu.VMEM((8, 64, 128), F32),
            pltpu.VMEM((8, 64, 128), F32),
            pltpu.VMEM((4096, 128), BF16),
            pltpu.VMEM((6, GRID, 8, 128), F32),
            pltpu.VMEM((6, GRID, 8, 128), F32),
            pltpu.VMEM((6, DP, 32, 128), F32),
            pltpu.VMEM((6, DP, 32, 128), F32),
            pltpu.VMEM((4, CO, 128), F32),
            pltpu.VMEM((4, 4, CO, 128), F32),
        ]
        + [sems(n) for n in (16, 10, 3, 6, 6, 6, 6, 4, 4)],
        compiler_params=params(collective_id=0),
    )(
        snapshots.reshape(8192, 128),
        cotangent.reshape(4096, 128),
        local_weight.T,
        spectral_weight.reshape(64, 4096),
        first_moment.reshape(64, 4096),
        second_moment.reshape(64, 4096),
        *tables,
    )
    named = dict(zip(TABLES, tables))
    grad_input, local_grad, new_weight, new_first, new_second = pl.pallas_call(
        last_kernel,
        out_shape=(shape((8192, 128), BF16), shape((CO, C), F32), state, state, state),
        in_specs=[vmem] + [hbm] * 2 + [vmem] + [hbm] * 3 + [vmem] * 2,
        out_specs=(hbm, vmem) + (hbm,) * 3,
        scratch_shapes=[
            pltpu.VMEM((4096, 128), F32),
            pltpu.VMEM((4, 256, 128), F32),
            pltpu.VMEM((4096, 128), BF16),
            pltpu.VMEM((4096, 128), BF16),
            pltpu.VMEM((64, 4096), F32),
            pltpu.VMEM((64, 4096), F32),
            pltpu.VMEM((64, 4096), F32),
            sems(5),
            sems(7),
        ],
        compiler_params=params(),
    )(last, back, half, local_grad, new_weight, new_first, new_second, named["y_inv"], named["z_inv"])
    return (
        grad_input.reshape(snapshots.shape),
        local_grad.T,
        new_weight.reshape(spectral_weight.shape),
        new_first.reshape(spectral_weight.shape),
        new_second.reshape(spectral_weight.shape),
    )


def solution(mesh):
    tables = make_tables()
    split_spec = P("dp", "grid", None)
    field_spec = P("dp", None, "grid", None, None)

    def step(*args):
        return on_device(tables, *args)

    return jax.shard_map(
        step,
        mesh=mesh,
        in_specs=(field_spec, field_spec, P(), split_spec, split_spec, split_spec),
        out_specs=(field_spec, P(), split_spec, split_spec, split_spec),
        check_vma=False,
    )
```

```python
import math

import jax
import jax.numpy as jnp
import ml_dtypes
import numpy as np
from jax import lax
from jax.experimental import pallas as pl
from jax.experimental.pallas import tpu as pltpu
from jax.sharding import PartitionSpec as P

NX = 128
NY = 64
NZ = 128
KX = 32
KY = 32
KZ = 16
STEP = 100
C = 64
CO = 32
GRID = 64
DP = 4
RATE = 0.02

MESH = pl.DeviceIdType.MESH
F32 = jnp.float32
BF16 = jnp.bfloat16
NN = (((1,), (0,)), ((), ()))
NT = (((1,), (1,)), ((), ()))


def mode_numbers(length, retained):
    a = np.arange(retained)
    return np.where(a < retained // 2, a, length - retained + a)


def angles(length, numbers):
    points = np.arange(length)
    return (points[:, None] * numbers[None, :] % length) * (2.0 * math.pi / length)


def rotation(theta, direction):
    cos, sin = np.cos(theta), direction * np.sin(theta)
    return np.stack([np.stack([cos, sin]), np.stack([-sin, cos])])


def split_table(table):
    high = table.astype(ml_dtypes.bfloat16)
    low = (table - high.astype(np.float64)).astype(ml_dtypes.bfloat16)
    return np.stack([high, low])


def make_tables():
    z_angles = angles(NZ, np.arange(KZ))
    fold = np.where(np.arange(KZ) == 0, 1.0, 2.0) / (NX * NY * NZ)
    z_fwd = np.concatenate([np.cos(z_angles).T, -np.sin(z_angles).T]).astype(ml_dtypes.bfloat16)
    z_fwd_scaled = (z_fwd.astype(np.float64) * np.tile(fold, 2)[:, None]).astype(ml_dtypes.bfloat16)
    z_inv = np.concatenate([np.cos(z_angles).T, -np.sin(z_angles).T])
    z_inv_scaled = z_inv * np.tile(fold, 2)[:, None]

    def four(table):
        out = np.zeros((4, 2 * KZ, 4, NZ))
        for j in range(4):
            out[j, :, j] = table
        return split_table(out.reshape(4 * 2 * KZ, 4 * NZ))

    y_theta = angles(NY, mode_numbers(NY, KY))
    x_theta = angles(NX, mode_numbers(NX, KX))
    y_rot = rotation(y_theta, -1.0)
    x_rot = rotation(x_theta, -1.0)
    x_rot = x_rot.reshape(2, 2, GRID, 2, DP, KX // DP)
    yi_rot = rotation(y_theta.T, 1.0)
    xi_rot = rotation(x_theta.T, 1.0)
    xi_rot = xi_rot.reshape(2, 2, DP, KX // DP, GRID, 2)
    y_fwd = np.zeros((KY, 2, 2, 2, 2, 2, 2, NY))
    x_fwd = np.zeros((DP, 2, 2, 8, GRID, 2, 2, 2))
    x_inv = np.zeros((GRID, 2, 2, 2, DP, 2, 2, 8))
    y_inv = np.zeros((KY, 2, 2, 2, 2, 2, 2, NY))
    for c in range(2):
        x_fwd[:, c, :, :, :, c] = x_rot.transpose(4, 1, 5, 2, 3, 0)
        x_inv[:, c, :, :, :, c] = xi_rot.transpose(4, 5, 1, 2, 0, 3)
        for x in range(2):
            y_fwd[:, c, x, :, c, :, x] = y_rot.transpose(3, 1, 0, 2)
            y_inv[:, c, x, :, c, :, x] = yi_rot.transpose(2, 0, 1, 3)
    spread = np.zeros((8, 16, 8, 16, 32))
    for q in range(8):
        for c in range(16):
            spread[q, c, q, c] = 1.0
    gather = np.zeros((8, 4, 32, 32, 8))
    for q in range(8):
        for o in range(32):
            gather[q, :, o, o, q] = 1.0
    return (
        z_fwd,
        z_fwd_scaled,
        four(z_inv_scaled),
        four(z_inv),
        split_table(y_fwd.reshape(256, 512)),
        split_table(x_fwd.reshape(128, 512)),
        split_table(x_inv.reshape(512, 128)),
        split_table(y_inv.reshape(256, 512)),
        spread.reshape(8, 128, 512).astype(ml_dtypes.bfloat16),
        gather.reshape(1024, 256).astype(ml_dtypes.bfloat16),
    )


def dot(a, b, dims=NN):
    return lax.dot_general(a, b, dims, preferred_element_type=F32)


def split(a):
    high = a.astype(BF16)
    return high, (a - high.astype(F32)).astype(BF16)


def table_dot(table, values, dims=NN):
    high, low = split(values)
    return dot(table[0], high, dims) + dot(table[0], low, dims) + dot(table[1], high, dims)


def dot_table(values, table):
    high, low = split(values)
    return dot(high, table[0]) + dot(low, table[0]) + dot(high, table[1])


def dot_exact(values, table, dims=NN):
    high, low = split(values)
    return dot(high, table, dims) + dot(low, table, dims)


def dp_and_grid():
    return lax.axis_index("dp"), lax.axis_index("grid")


def inverse_y(recv, table, ub):
    for h in range(2):
        values = recv[h * 32 : (h + 1) * 32].reshape(256, 128).T
        result = dot_table(values, table)
        for j in range(4):
            ub[j, h * 128 : (h + 1) * 128, :] = result[:, j * 128 : (j + 1) * 128]


def inverse_z(ub, table, c, finish):
    def body(i, _):
        groups = []
        for g in range(2):
            row = i * 64 + g * 32
            parts = [
                ub[c * 2 + s, pl.ds(row + h * 128 + j * 8, 8), :]
                for j in range(4) for s in range(2) for h in range(2)
            ]
            groups.append(jnp.concatenate(parts, axis=0).T)
        result = dot_table(jnp.concatenate(groups, axis=0), table)
        for g in range(2):
            for j in range(4):
                finish(
                    pl.ds(c * 2048 + i * 1024 + g * 512 + j * 128, 128),
                    result[g * 128 : (g + 1) * 128, j * 128 : (j + 1) * 128],
                )
        return 0

    lax.fori_loop(0, 2, body, 0)


TABLES = (
    "z_fwd", "z_fwd_scaled", "z_inv_scaled", "z_inv", "y_fwd", "x_fwd", "x_inv", "y_inv", "spread", "gather"
)


def kernel(
    snap_hbm, cot_hbm, lw_hbm, weight_hbm, first_hbm, second_hbm,
    z_fwd_hbm, z_fwd_scaled_hbm, z_inv_scaled_hbm, z_inv_hbm, y_fwd_hbm, x_fwd_hbm, x_inv_hbm, y_inv_hbm,
    spread_hbm, gather_hbm,
    last_hbm, back_hbm, half_hbm, local_out, new_weight_hbm, new_first_hbm, new_second_hbm,
    snap, cot, lw_t, z_fwd, z_fwd_scaled, z_inv_scaled, z_inv, y_fwd, x_fwd, x_inv, y_inv, spread, gather,
    weight, first, second, new_weight, new_first, new_second,
    zb, snap_f, pre, back_a, back_b, grad_b, grad_f, ub, spec_x, mixed, grad_x, half,
    gsend, grecv, dsend, drecv, lsend, lrecv,
    load_sems, state_sems, out_sems, gsend_sems, grecv_sems, dsend_sems, drecv_sems, lsend_sems, lrecv_sems,
):
    d, me = dp_and_grid()
    slot_of = lambda g: lax.rem(g, 2) * 32 + lax.div(g, 2)
    place = lambda g: g
    pending, stored = [], []

    barrier = pltpu.get_barrier_semaphore()

    def greet_grid(i, _):
        pl.semaphore_signal(barrier, inc=1, device_id={"grid": lax.rem(me + i, GRID)}, device_id_type=MESH)
        return 0

    def greet_dp(i, _):
        pl.semaphore_signal(barrier, inc=1, device_id={"dp": lax.rem(d + i, DP)}, device_id_type=MESH)
        return 0

    lax.fori_loop(1, DP, greet_dp, 0)

    loads = {}

    def load(name, src, dst):
        copy = pltpu.make_async_copy(src, dst, load_sems.at[len(loads)])
        copy.start()
        loads[name] = copy

    def need(*names):
        for name in names:
            loads.pop(name).wait()

    def snap_rows(t, c):
        return pl.ds(c * 4096 + t * 2048, 2048)

    def load_snap(t, c, n):
        rows = snap_rows(t, c)
        return pltpu.make_async_copy(snap_hbm.at[rows], snap.at[rows], state_sems.at[n])

    load("z_fwd", z_fwd_hbm, z_fwd)
    load_snap(0, 0, 6).start()
    load_snap(0, 1, 7).start()
    load("y_fwd", y_fwd_hbm, y_fwd)
    load_snap(1, 0, 8).start()
    load_snap(1, 1, 9).start()

    lax.fori_loop(1, GRID, greet_grid, 0)

    load("x_fwd", x_fwd_hbm, x_fwd)
    load("spread", spread_hbm, spread)

    def load_state(n, src, dst):
        pltpu.make_async_copy(src, dst, state_sems.at[n]).start()

    def need_state(n, dst):
        pltpu.make_async_copy(dst, dst, state_sems.at[n]).wait()

    load_state(0, weight_hbm, weight)
    load("gather", gather_hbm, gather)
    load("lw", lw_hbm, lw_t)
    load("x_inv", x_inv_hbm, x_inv)
    load("y_inv", y_inv_hbm, y_inv)
    load("z_inv_scaled", z_inv_scaled_hbm, z_inv_scaled)
    load("cot", cot_hbm, cot)
    load("z_fwd_scaled", z_fwd_scaled_hbm, z_fwd_scaled)
    load_state(1, first_hbm, first)
    load_state(2, second_hbm, second)
    load("z_inv", z_inv_hbm, z_inv)

    def grid_send(n, src_slot, dst_slot):
        def body(i, _):
            to = lax.rem(me + i, GRID)
            pltpu.make_async_remote_copy(
                src_ref=gsend.at[n, src_slot(to)],
                dst_ref=grecv.at[n, dst_slot(me)],
                send_sem=gsend_sems.at[n],
                recv_sem=grecv_sems.at[n],
                device_id={"grid": to},
                device_id_type=MESH,
            ).start()
            return 0

        lax.fori_loop(1, GRID, body, 0)
        grecv[n, dst_slot(me)] = gsend[n, src_slot(me)]
        pending.append((gsend_sems, n, gsend.at[n]))

    near = lax.div(d, 2)
    far = 1 - near
    core = lax.rem(d, 2)

    def dp_copy(n, sem, to):
        pltpu.make_async_remote_copy(
            src_ref=dsend.at[n, to],
            dst_ref=drecv.at[n, d],
            send_sem=dsend_sems.at[sem],
            recv_sem=drecv_sems.at[sem],
            device_id={"dp": to},
            device_id_type=MESH,
        ).start()

    def send_far(n):
        for i in range(2):
            dp_copy(n, n, far * 2 + lax.rem(core + i, 2))
        pending.append((dsend_sems, n, dsend.at[n, pl.ds(0, 3)]))

    def send_near(n):
        dp_copy(n, 6 + n, near * 2 + 1 - core)
        drecv[n, d] = dsend[n, d]
        pending.append((dsend_sems, 6 + n, dsend.at[n, pl.ds(0, 2)]))

    def wait_all(sems, n, ref):
        part = ref.at[pl.ds(0, ref.shape[0] - 1)]
        pltpu.make_async_copy(part, part, sems.at[n]).wait()

    def grid_wait(n):
        wait_all(grecv_sems, n, grecv.at[n])

    def wait_far(n):
        wait_all(drecv_sems, n, drecv.at[n, pl.ds(0, 3)])

    def wait_near(n):
        wait_all(drecv_sems, 6 + n, drecv.at[n, pl.ds(0, 2)])

    def forward_z(field, row_of, table, c):
        for part in range(2):
            start = row_of(c) + part * 1024
            z = dot(table[...], field[pl.ds(start, 1024), :], NT)
            for r in range(2):
                for h in range(2):
                    for j in range(8):
                        row = h * 128 + (part * 8 + j) * 8
                        zb[c * 2 + r, row : row + 8, :] = z[
                            (r * 2 + h) * 8 : (r * 2 + h + 1) * 8, j * 128 : (j + 1) * 128
                        ]

    def forward_y(n):
        for h in range(2):
            values = jnp.concatenate([zb[j, h * 128 : (h + 1) * 128, :] for j in range(4)], axis=1)
            result = table_dot(y_fwd, values, NT)
            gsend[n, h * 32 : (h + 1) * 32] = result.reshape(32, 8, 128)

    def forward_x(n, m):
        result = table_dot(x_fwd, grecv[n].reshape(512, 128))
        dsend[m] = result.reshape(DP, 32, 128)

    def inverse_x(m, n):
        result = table_dot(x_inv, drecv[m].reshape(128, 128))
        gsend[n] = result.reshape(GRID, 8, 128)

    need("z_fwd")
    for t in range(2):
        for c in range(2):
            load_snap(t, c, 6 + t * 2 + c).wait()
            forward_z(snap, lambda c: c * 4096 + t * 2048, z_fwd, c)
        if t == 0:
            need("y_fwd")
        forward_y(t)
        if t == 0:
            pl.semaphore_wait(barrier, GRID - 1 + DP - 1)
        grid_send(t, slot_of, place)

    def widen(i, _):
        rows = pl.ds(i * 512, 512)
        snap_f[rows, :] = snap[rows, :].astype(F32)
        return 0

    lax.fori_loop(0, 16, widen, 0)

    need("x_fwd")
    for t in range(2):
        grid_wait(t)
        forward_x(t, t)
        send_far(t)
        send_near(t)

    def w_tiles(r, c, t):
        return range(r * 16 + c * 8 + t * 4, r * 16 + c * 8 + t * 4 + 4)

    def w_read(ref, q, r, c, t):
        return jnp.concatenate([ref[pl.ds(j * 8 + q, 8, stride=256), :] for j in w_tiles(r, c, t)], axis=1)

    def w_write(ref, q, r, c, t, value):
        for n, j in enumerate(w_tiles(r, c, t)):
            ref[pl.ds(j * 8 + q, 8, stride=256), :] = value[:, n * 128 : (n + 1) * 128]

    def s_rows(t, s, c, r):
        return pl.ds(((t * 4 + s) * 2 + c) * 16 + r * 8, 8)

    def mix(t, side):
        high, low = split(drecv[t, pl.ds(side * 2, 2)].reshape(64, 128))

        def body(q, _):
            spectra = dot(high, spread[q]) + dot(low, spread[q])
            spec_x[q, pl.ds(pl.multiple_of(t * 128 + side * 64, 64), 64)] = spectra
            if t == 0:
                sums = [[jnp.zeros((8, 128), F32) for _ in range(2)] for _ in range(2)]
            else:
                sums = [[mixed[q, side * 2 + s, r * 8 : (r + 1) * 8, :] for r in range(2)] for s in range(2)]
            for c in range(2):
                w_re, w_im = w_read(weight, q, 0, c, t), w_read(weight, q, 1, c, t)
                for s in range(2):
                    row = (s * 2 + c) * 16
                    s_re, s_im = spectra[row : row + 8], spectra[row + 8 : row + 16]
                    products = (s_re * w_re - s_im * w_im, s_re * w_im + s_im * w_re)
                    for r in range(2):
                        for j in range(4):
                            sums[s][r] = sums[s][r] + products[r][:, j * 128 : (j + 1) * 128]
            for s in range(2):
                for r in range(2):
                    mixed[q, side * 2 + s, r * 8 : (r + 1) * 8, :] = sums[s][r]
            return 0

        lax.fori_loop(0, 8, body, 0, unroll=2)

    need("spread")
    need_state(0, weight)
    for t in range(2):
        wait_near(t)
        mix(t, near)
        wait_far(t)
        mix(t, far)
    need("gather")
    values = jnp.concatenate([mixed[q].reshape(64, 128) for q in range(8)], axis=1)
    result = dot_exact(values, gather[...])
    for c in range(2):
        dsend[2, :, c * 16 : (c + 1) * 16, :] = result[:, c * 128 : (c + 1) * 128].reshape(4, 16, 128)
    send_far(2)
    send_near(2)
    need("x_inv")
    wait_near(2)
    wait_far(2)

    inverse_x(2, 2)
    grid_send(2, place, slot_of)

    def strided(ref, cell, channels):
        return jnp.concatenate(
            [ref[pl.ds(cell * 4 + j, channels, stride=128), :] for j in range(4)], axis=1
        ).astype(BF16)

    def local_forward(i, _):
        result = dot(lw_t[...], strided(snap_f, i, C))
        for j in range(4):
            pre[pl.ds(i * 4 + j, CO, stride=128), :] = result[:, j * 128 : (j + 1) * 128]
        return 0

    need("lw")
    lax.fori_loop(0, 32, local_forward, 0, unroll=4)
    lw = lw_t[...].astype(F32).T.astype(BF16)
    need("y_inv", "z_inv_scaled", "cot")
    grid_wait(2)

    inverse_y(grecv.at[2], y_inv, ub)

    def through_gelu(rows, spectral):
        v = spectral + pre[rows, :]
        k = math.sqrt(2.0 / math.pi)
        square = v * v
        t = jnp.tanh(v * (k + (k * 0.044715) * square))
        bend = v * (0.5 * k + (1.5 * k * 0.044715) * square)
        slope = (0.5 + 0.5 * t) + bend * (1.0 - t * t)
        grad_b[rows, :] = (cot[rows, :].astype(F32) * slope).astype(BF16)

    need("z_fwd_scaled")
    for c in range(2):
        inverse_z(ub, z_inv_scaled, c, through_gelu)
        forward_z(grad_b, lambda c: c * 2048, z_fwd_scaled, c)
    forward_y(3)
    grid_send(3, slot_of, place)

    lsend[...] = jnp.zeros_like(lsend)

    def widen_grad(i, _):
        rows = pl.ds(i * 512, 512)
        grad_f[rows, :] = grad_b[rows, :].astype(F32)
        return 0

    lax.fori_loop(0, 8, widen_grad, 0)

    def local_grad(i, total):
        return total + dot(strided(grad_f, i, CO), strided(snap_f, i, C), NT)

    total = lax.fori_loop(0, 32, local_grad, jnp.zeros((CO, C), F32), unroll=4)
    gx, gz, gy = lax.div(me, 16), lax.rem(lax.div(me, 4), 4), lax.rem(me, 4)
    rounds = (
        (gy, lambda j: {"grid": me - gy + j}),
        (gz, lambda j: {"grid": me - 4 * gz + 4 * j}),
        (gx, lambda j: {"grid": me - 16 * gx + 16 * j}),
        (d, lambda j: {"dp": j}),
    )

    def local_send(n, value):
        mine, device = rounds[n]
        lsend[n, :, 0:C] = value

        def body(i, _):
            pltpu.make_async_remote_copy(
                src_ref=lsend.at[n],
                dst_ref=lrecv.at[n, mine],
                send_sem=lsend_sems.at[n],
                recv_sem=lrecv_sems.at[n],
                device_id=device(lax.rem(mine + i, 4)),
                device_id_type=MESH,
            ).start()
            return 0

        lax.fori_loop(1, 4, body, 0)
        lrecv[n, mine] = lsend[n]
        pending.append((lsend_sems, n, lrecv.at[n]))

    def local_sum(n):
        wait_all(lrecv_sems, n, lrecv.at[n])
        return ((lrecv[n, 0] + lrecv[n, 1]) + (lrecv[n, 2] + lrecv[n, 3]))[:, 0:C]

    local_send(0, total)

    def local_backward(i, _):
        result = dot(lw, strided(grad_f, i, CO))
        for j in range(4):
            for c in range(2):
                for t, ref in enumerate((back_a, back_b)):
                    row = c * 32 + t * 16
                    ref[pl.ds(c * 2048 + i * 4 + j, 16, stride=128), :] = result[
                        row : row + 16, j * 128 : (j + 1) * 128
                    ]
        return 0

    def store(n, src, dst):
        copy = pltpu.make_async_copy(src, dst, out_sems.at[n])
        copy.start()
        stored.append(copy)

    lax.fori_loop(0, 12, local_backward, 0, unroll=4)
    grid_wait(3)

    forward_x(3, 3)
    send_far(3)
    send_near(3)
    local_send(1, local_sum(0))

    def spread_gradients(side):
        rows = pl.ds(side * 2, 2)
        values = jnp.concatenate(
            [drecv[3, rows, c * 16 : (c + 1) * 16, :].reshape(32, 128) for c in range(2)], axis=1
        )
        result = dot_exact(values, gather[...], NT)
        for q in range(8):
            grad_x[q, rows] = result[:, q * 128 : (q + 1) * 128].reshape(2, 16, 128)

    def g_tile(q, s, r):
        return jnp.concatenate([grad_x[q, s, r * 8 : (r + 1) * 8, :]] * 4, axis=1)

    def input_modes(t, side):
        def body(q, total):
            parts = {}
            for c in range(2):
                w_re, w_im = w_read(weight, q, 0, c, t), w_read(weight, q, 1, c, t)
                for s in range(2):
                    g_re, g_im = g_tile(q, side * 2 + s, 0), g_tile(q, side * 2 + s, 1)
                    parts[s, c, 0] = w_re * g_re + w_im * g_im
                    parts[s, c, 1] = w_re * g_im - w_im * g_re
            values = jnp.concatenate(
                [parts[s, c, r] for s in range(2) for c in range(2) for r in range(2)], axis=0
            )
            return total + dot_exact(values, spread[q], NT)

        total = lax.fori_loop(0, 8, body, jnp.zeros((64, 128), F32), unroll=2)
        dsend[4 + t, pl.ds(side * 2, 2)] = total.reshape(2, 32, 128)

    wait_near(3)
    spread_gradients(near)
    for t in range(2):
        input_modes(t, near)
        send_near(4 + t)
    wait_far(3)
    spread_gradients(far)
    for t in range(2):
        input_modes(t, far)
        send_far(4 + t)
    local_send(2, local_sum(1))
    lax.fori_loop(12, 32, local_backward, 0, unroll=4)
    store(0, back_b, back_hbm)
    local_send(3, local_sum(2))

    need_state(1, first)
    need_state(2, second)

    def adam(q, _):
        for c in range(2):
            for t in range(2):
                re = im = None
                for s in range(4):
                    s_re = spec_x[q, s_rows(t, s, c, 0), :]
                    s_im = spec_x[q, s_rows(t, s, c, 1), :]
                    g_re, g_im = g_tile(q, s, 0), g_tile(q, s, 1)
                    a, b = s_re * g_re + s_im * g_im, s_re * g_im - s_im * g_re
                    re, im = (a, b) if re is None else (re + a, im + b)
                for r, g in enumerate((re, im)):
                    m = 0.9 * w_read(first, q, r, c, t) + 0.1 * g
                    v = 0.999 * w_read(second, q, r, c, t) + 0.001 * g * g
                    step = (m / (1.0 - 0.9**STEP)) / (jnp.sqrt(v / (1.0 - 0.999**STEP)) + 1e-8)
                    w_write(new_first, q, r, c, t, m)
                    w_write(new_second, q, r, c, t, v)
                    w_write(new_weight, q, r, c, t, w_read(weight, q, r, c, t) - RATE * step)
        return 0

    for t in range(2):
        wait_near(4 + t)
        wait_far(4 + t)
        inverse_x(4 + t, 4 + t)
        grid_send(4 + t, place, slot_of)
    lax.fori_loop(0, 8, adam, 0)
    states = ((new_weight, new_weight_hbm), (new_first, new_first_hbm), (new_second, new_second_hbm))

    for n, (src, dst) in enumerate(states):
        store(3 + n, src, dst)
    need("z_inv")
    grid_wait(4)
    inverse_y(grecv.at[4], y_inv, ub)

    def finish(rows, spectral):
        half[rows, :] = (spectral + back_a[rows, :]).astype(BF16)

    for c in range(2):
        inverse_z(ub, z_inv, c, finish)
    store(1, half, half_hbm)
    local_out[...] = local_sum(3)
    grid_wait(5)
    store(2, grecv.at[5], last_hbm)

    for sems, n, ref in pending:
        wait_all(sems, n, ref)
    for copy in stored:
        copy.wait()


def last_kernel(
    last_hbm, back_hbm, half_hbm, local, weight_hbm, first_hbm, second_hbm, y_inv_hbm, z_inv_hbm,
    out_hbm, local_out, new_weight_hbm, new_first_hbm, new_second_hbm,
    last, back, y_inv, z_inv, ub, half, half_a, weight, first, second, in_sems, out_sems,
):
    sources = (last_hbm, y_inv_hbm, z_inv_hbm, back_hbm, half_hbm, weight_hbm, first_hbm, second_hbm)
    places = (last, y_inv, z_inv, back, half_a, weight, first, second)
    loads = [pltpu.make_async_copy(a, b, in_sems.at[n]) for n, (a, b) in enumerate(zip(sources, places))]
    for copy in loads:
        copy.start()
    stores = []

    def store(src, dst):
        copy = pltpu.make_async_copy(src, dst, out_sems.at[len(stores)])
        copy.start()
        stores.append(copy)

    def finish(rows, spectral):
        half[rows, :] = (spectral + back[rows, :]).astype(BF16)

    def store_half(src, t, c):
        store(src.at[pl.ds(c * 2048, 2048)], out_hbm.at[pl.ds(c * 4096 + t * 2048, 2048)])

    local_out[...] = local[...]
    loads[0].wait()
    loads[1].wait()
    inverse_y(last, y_inv, ub)
    loads[2].wait()
    loads[3].wait()
    inverse_z(ub, z_inv, 0, finish)
    store_half(half, 1, 0)
    loads[4].wait()
    for c in range(2):
        store_half(half_a, 0, c)
    for copy, src, dst in zip(loads[5:], places[5:], (new_weight_hbm, new_first_hbm, new_second_hbm)):
        copy.wait()
        store(src, dst)
    inverse_z(ub, z_inv, 1, finish)
    store_half(half, 1, 1)
    for copy in stores:
        copy.wait()


def to_rows(state):
    return state.reshape(8, 8, 32, 128).transpose(0, 2, 1, 3).reshape(2048, 128)


def from_rows(rows):
    return rows.reshape(8, 32, 8, 128).transpose(0, 2, 1, 3).reshape(8, 8, 4096)


def on_device(tables, snapshots, cotangent, local_weight, spectral_weight, first_moment, second_moment):
    vmem = pl.BlockSpec(memory_space=pltpu.VMEM)
    hbm = pl.BlockSpec(memory_space=pl.ANY)
    shape = jax.ShapeDtypeStruct
    state = shape((2048, 128), F32)
    state_scratch = pltpu.VMEM((2048, 128), F32)
    sems = lambda n: pltpu.SemaphoreType.DMA((n,))
    table_scratch = [pltpu.VMEM(table.shape, BF16) for table in tables]
    params = lambda **more: pltpu.CompilerParams(
        has_side_effects=True, vmem_limit_bytes=56 * 1024 * 1024, **more
    )
    last, back, half, local_grad, new_weight, new_first, new_second = pl.pallas_call(
        kernel,
        out_shape=(
            shape((GRID, 8, 128), F32), shape((4096, 128), F32), shape((4096, 128), BF16), shape((CO, C), F32),
            state, state, state,
        ),
        in_specs=[hbm] * (6 + len(tables)),
        out_specs=(hbm,) * 3 + (vmem,) + (hbm,) * 3,
        scratch_shapes=[
            pltpu.VMEM((8192, 128), BF16),
            pltpu.VMEM((4096, 128), BF16),
            pltpu.VMEM((CO, C), BF16),
        ]
        + table_scratch
        + [state_scratch] * 6
        + [
            pltpu.VMEM((4, 256, 128), F32),
            pltpu.VMEM((8192, 128), F32),
            pltpu.VMEM((4096, 128), F32),
            pltpu.VMEM((4096, 128), F32),
            pltpu.VMEM((4096, 128), F32),
            pltpu.VMEM((4096, 128), BF16),
            pltpu.VMEM((4096, 128), F32),
            pltpu.VMEM((4, 256, 128), F32),
            pltpu.VMEM((8, 256, 512), F32),
            pltpu.VMEM((8, 4, 16, 128), F32),
            pltpu.VMEM((8, 4, 16, 128), F32),
            pltpu.VMEM((4096, 128), BF16),
            pltpu.VMEM((6, GRID, 8, 128), F32),
            pltpu.VMEM((6, GRID, 8, 128), F32),
            pltpu.VMEM((6, DP, 32, 128), F32),
            pltpu.VMEM((6, DP, 32, 128), F32),
            pltpu.VMEM((4, CO, 128), F32),
            pltpu.VMEM((4, 4, CO, 128), F32),
        ]
        + [sems(n) for n in (16, 10, 6, 6, 6, 12, 12, 4, 4)],
        compiler_params=params(collective_id=0),
    )(
        snapshots.reshape(8192, 128),
        cotangent.reshape(4096, 128),
        local_weight.T,
        to_rows(spectral_weight),
        to_rows(first_moment),
        to_rows(second_moment),
        *tables,
    )
    named = dict(zip(TABLES, tables))
    grad_input, local_grad, new_weight, new_first, new_second = pl.pallas_call(
        last_kernel,
        out_shape=(shape((8192, 128), BF16), shape((CO, C), F32), state, state, state),
        in_specs=[hbm] * 3 + [vmem] + [hbm] * 5,
        out_specs=(hbm, vmem) + (hbm,) * 3,
        scratch_shapes=[
            pltpu.VMEM((GRID, 8, 128), F32),
            pltpu.VMEM((4096, 128), F32),
            pltpu.VMEM(named["y_inv"].shape, BF16),
            pltpu.VMEM(named["z_inv"].shape, BF16),
            pltpu.VMEM((4, 256, 128), F32),
            pltpu.VMEM((4096, 128), BF16),
            pltpu.VMEM((4096, 128), BF16),
        ]
        + [state_scratch] * 3
        + [sems(8), sems(7)],
        compiler_params=params(),
    )(last, back, half, local_grad, new_weight, new_first, new_second, named["y_inv"], named["z_inv"])
    return (
        grad_input.reshape(snapshots.shape),
        local_grad.T,
        from_rows(new_weight),
        from_rows(new_first),
        from_rows(new_second),
    )


def solution(mesh):
    tables = make_tables()
    split_spec = P("dp", "grid", None)
    field_spec = P("dp", None, "grid", None, None)

    def step(*args):
        return on_device(tables, *args)

    return jax.shard_map(
        step,
        mesh=mesh,
        in_specs=(field_spec, field_spec, P(), split_spec, split_spec, split_spec),
        out_specs=(field_spec, P(), split_spec, split_spec, split_spec),
        check_vma=False,
    )
```

```python
import math

import jax
import jax.numpy as jnp
import ml_dtypes
import numpy as np
from jax import lax
from jax.experimental import pallas as pl
from jax.experimental.pallas import tpu as pltpu
from jax.sharding import PartitionSpec as P

NX = 128
NY = 64
NZ = 128
KX = 32
KY = 32
KZ = 16
STEP = 100
C = 64
CO = 32
GRID = 64
DP = 4
RATE = 0.02

MESH = pl.DeviceIdType.MESH
F32 = jnp.float32
BF16 = jnp.bfloat16
NN = (((1,), (0,)), ((), ()))
NT = (((1,), (1,)), ((), ()))


def mode_numbers(length, retained):
    a = np.arange(retained)
    return np.where(a < retained // 2, a, length - retained + a)


def angles(length, numbers):
    points = np.arange(length)
    return (points[:, None] * numbers[None, :] % length) * (2.0 * math.pi / length)


def rotation(theta, direction):
    cos, sin = np.cos(theta), direction * np.sin(theta)
    return np.stack([np.stack([cos, sin]), np.stack([-sin, cos])])


def split_table(table):
    high = table.astype(ml_dtypes.bfloat16)
    low = (table - high.astype(np.float64)).astype(ml_dtypes.bfloat16)
    return np.stack([high, low])


def make_tables():
    z_angles = angles(NZ, np.arange(KZ))
    fold = np.where(np.arange(KZ) == 0, 1.0, 2.0) / (NX * NY * NZ)
    z_fwd = np.concatenate([np.cos(z_angles).T, -np.sin(z_angles).T]).astype(ml_dtypes.bfloat16)
    z_fwd_scaled = (z_fwd.astype(np.float64) * np.tile(fold, 2)[:, None]).astype(ml_dtypes.bfloat16)
    z_inv = np.concatenate([np.cos(z_angles).T, -np.sin(z_angles).T])
    z_inv_scaled = z_inv * np.tile(fold, 2)[:, None]

    def four(table):
        out = np.zeros((4, 2 * KZ, 4, NZ))
        for j in range(4):
            out[j, :, j] = table
        return split_table(out.reshape(4 * 2 * KZ, 4 * NZ))

    y_theta = angles(NY, mode_numbers(NY, KY))
    x_theta = angles(NX, mode_numbers(NX, KX))
    y_rot = rotation(y_theta, -1.0)
    x_rot = rotation(x_theta, -1.0)
    x_rot = x_rot.reshape(2, 2, GRID, 2, DP, KX // DP)
    yi_rot = rotation(y_theta.T, 1.0)
    xi_rot = rotation(x_theta.T, 1.0)
    xi_rot = xi_rot.reshape(2, 2, DP, KX // DP, GRID, 2)
    y_fwd = np.zeros((KY, 2, 2, 2, 2, 2, 2, NY))
    x_fwd = np.zeros((DP, 2, 2, 8, GRID, 2, 2, 2))
    x_inv = np.zeros((GRID, 2, 2, 2, DP, 2, 2, 8))
    y_inv = np.zeros((KY, 2, 2, 2, 2, 2, 2, NY))
    for c in range(2):
        x_fwd[:, c, :, :, :, c] = x_rot.transpose(4, 1, 5, 2, 3, 0)
        x_inv[:, c, :, :, :, c] = xi_rot.transpose(4, 5, 1, 2, 0, 3)
        for x in range(2):
            y_fwd[:, c, x, :, c, :, x] = y_rot.transpose(3, 1, 0, 2)
            y_inv[:, c, x, :, c, :, x] = yi_rot.transpose(2, 0, 1, 3)
    spread = np.zeros((8, 16, 8, 16, 32))
    for q in range(8):
        for c in range(16):
            spread[q, c, q, c] = 1.0
    gather = np.zeros((8, 4, 32, 32, 8))
    for q in range(8):
        for o in range(32):
            gather[q, :, o, o, q] = 1.0
    return (
        z_fwd,
        z_fwd_scaled,
        four(z_inv_scaled),
        four(z_inv),
        split_table(y_fwd.reshape(256, 512)),
        split_table(x_fwd.reshape(128, 512)),
        split_table(x_inv.reshape(512, 128)),
        split_table(y_inv.reshape(256, 512)),
        spread.reshape(8, 128, 512).astype(ml_dtypes.bfloat16),
        gather.reshape(1024, 256).astype(ml_dtypes.bfloat16),
    )


def dot(a, b, dims=NN):
    return lax.dot_general(a, b, dims, preferred_element_type=F32)


def split(a):
    high = a.astype(BF16)
    return high, (a - high.astype(F32)).astype(BF16)


def table_dot(table, values, dims=NN):
    high, low = split(values)
    return dot(table[0], high, dims) + dot(table[0], low, dims) + dot(table[1], high, dims)


def dot_table(values, table):
    high, low = split(values)
    return dot(high, table[0]) + dot(low, table[0]) + dot(high, table[1])


def dot_exact(values, table, dims=NN):
    high, low = split(values)
    return dot(high, table, dims) + dot(low, table, dims)


def dp_and_grid():
    return lax.axis_index("dp"), lax.axis_index("grid")


def inverse_y(recv, table, ub):
    for h in range(2):
        values = recv[h * 32 : (h + 1) * 32].reshape(256, 128).T
        result = dot_table(values, table)
        for j in range(4):
            ub[j, h * 128 : (h + 1) * 128, :] = result[:, j * 128 : (j + 1) * 128]


def inverse_z(ub, table, c, finish):
    def body(i, _):
        groups = []
        for g in range(2):
            row = i * 64 + g * 32
            parts = [
                ub[c * 2 + s, pl.ds(row + h * 128 + j * 8, 8), :]
                for j in range(4) for s in range(2) for h in range(2)
            ]
            groups.append(jnp.concatenate(parts, axis=0).T)
        result = dot_table(jnp.concatenate(groups, axis=0), table)
        for g in range(2):
            for j in range(4):
                finish(
                    pl.ds(c * 2048 + i * 1024 + g * 512 + j * 128, 128),
                    result[g * 128 : (g + 1) * 128, j * 128 : (j + 1) * 128],
                )
        return 0

    lax.fori_loop(0, 2, body, 0, unroll=2)


TABLES = (
    "z_fwd", "z_fwd_scaled", "z_inv_scaled", "z_inv", "y_fwd", "x_fwd", "x_inv", "y_inv", "spread", "gather"
)


def kernel(
    snap_hbm, cot_hbm, lw_hbm, weight_hbm, first_hbm, second_hbm,
    z_fwd_hbm, z_fwd_scaled_hbm, z_inv_scaled_hbm, z_inv_hbm, y_fwd_hbm, x_fwd_hbm, x_inv_hbm, y_inv_hbm,
    spread_hbm, gather_hbm,
    last_hbm, back_hbm, half_hbm, local_out, new_weight_hbm, new_first_hbm, new_second_hbm,
    snap, cot, lw_t, z_fwd, z_fwd_scaled, z_inv_scaled, z_inv, y_fwd, x_fwd, x_inv, y_inv, spread, gather,
    weight, first, second, new_weight, new_first, new_second,
    zb, snap_f, pre, back_a, back_b, grad_b, grad_f, ub, spec_x, mixed, grad_x, half,
    gsend, grecv, dsend, drecv, lsend, lrecv,
    load_sems, state_sems, out_sems, gsend_sems, grecv_sems, dsend_sems, drecv_sems, lsend_sems, lrecv_sems,
):
    d, me = dp_and_grid()
    slot_of = lambda g: lax.rem(g, 2) * 32 + lax.div(g, 2)
    place = lambda g: g
    pending, stored = [], []

    barrier = pltpu.get_barrier_semaphore()

    def greet_grid(i, _):
        pl.semaphore_signal(barrier, inc=1, device_id={"grid": lax.rem(me + i, GRID)}, device_id_type=MESH)
        return 0

    def greet_dp(i, _):
        pl.semaphore_signal(barrier, inc=1, device_id={"dp": lax.rem(d + i, DP)}, device_id_type=MESH)
        return 0

    lax.fori_loop(1, DP, greet_dp, 0)

    loads = {}

    def load(name, src, dst):
        copy = pltpu.make_async_copy(src, dst, load_sems.at[len(loads)])
        copy.start()
        loads[name] = copy

    def need(*names):
        for name in names:
            loads.pop(name).wait()

    def snap_rows(t, c):
        return pl.ds(c * 4096 + t * 2048, 2048)

    def load_snap(t, c, n):
        rows = snap_rows(t, c)
        return pltpu.make_async_copy(snap_hbm.at[rows], snap.at[rows], state_sems.at[n])

    load("z_fwd", z_fwd_hbm, z_fwd)
    load_snap(0, 0, 6).start()
    load_snap(0, 1, 7).start()
    load("y_fwd", y_fwd_hbm, y_fwd)
    load_snap(1, 0, 8).start()
    load_snap(1, 1, 9).start()

    lax.fori_loop(1, GRID, greet_grid, 0)

    load("x_fwd", x_fwd_hbm, x_fwd)
    load("spread", spread_hbm, spread)

    def load_state(n, src, dst):
        pltpu.make_async_copy(src, dst, state_sems.at[n]).start()

    def need_state(n, dst):
        pltpu.make_async_copy(dst, dst, state_sems.at[n]).wait()

    load_state(0, weight_hbm, weight)
    load("gather", gather_hbm, gather)
    load("lw", lw_hbm, lw_t)
    load("x_inv", x_inv_hbm, x_inv)
    load("y_inv", y_inv_hbm, y_inv)
    load("z_inv_scaled", z_inv_scaled_hbm, z_inv_scaled)
    load("cot", cot_hbm, cot)
    load("z_fwd_scaled", z_fwd_scaled_hbm, z_fwd_scaled)
    load_state(1, first_hbm, first)
    load_state(2, second_hbm, second)
    load("z_inv", z_inv_hbm, z_inv)

    def grid_send(n, src_slot, dst_slot):
        def body(i, _):
            to = lax.rem(me + i, GRID)
            pltpu.make_async_remote_copy(
                src_ref=gsend.at[n, src_slot(to)],
                dst_ref=grecv.at[n, dst_slot(me)],
                send_sem=gsend_sems.at[n],
                recv_sem=grecv_sems.at[n],
                device_id={"grid": to},
                device_id_type=MESH,
            ).start()
            return 0

        lax.fori_loop(1, GRID, body, 0)
        grecv[n, dst_slot(me)] = gsend[n, src_slot(me)]
        pending.append((gsend_sems, n, gsend.at[n]))

    near = lax.div(d, 2)
    far = 1 - near
    core = lax.rem(d, 2)

    def dp_copy(n, sem, to):
        pltpu.make_async_remote_copy(
            src_ref=dsend.at[n, to],
            dst_ref=drecv.at[n, d],
            send_sem=dsend_sems.at[sem],
            recv_sem=drecv_sems.at[sem],
            device_id={"dp": to},
            device_id_type=MESH,
        ).start()

    def send_far(n):
        for i in range(2):
            dp_copy(n, n, far * 2 + lax.rem(core + i, 2))
        pending.append((dsend_sems, n, dsend.at[n, pl.ds(0, 3)]))

    def send_near(n):
        dp_copy(n, 6 + n, near * 2 + 1 - core)
        drecv[n, d] = dsend[n, d]
        pending.append((dsend_sems, 6 + n, dsend.at[n, pl.ds(0, 2)]))

    def wait_all(sems, n, ref):
        part = ref.at[pl.ds(0, ref.shape[0] - 1)]
        pltpu.make_async_copy(part, part, sems.at[n]).wait()

    def grid_wait(n):
        wait_all(grecv_sems, n, grecv.at[n])

    def wait_far(n):
        wait_all(drecv_sems, n, drecv.at[n, pl.ds(0, 3)])

    def wait_near(n):
        wait_all(drecv_sems, 6 + n, drecv.at[n, pl.ds(0, 2)])

    def forward_z(field, row_of, table, c):
        for part in range(2):
            start = row_of(c) + part * 1024
            z = dot(table[...], field[pl.ds(start, 1024), :], NT)
            for r in range(2):
                for h in range(2):
                    for j in range(8):
                        row = h * 128 + (part * 8 + j) * 8
                        zb[c * 2 + r, row : row + 8, :] = z[
                            (r * 2 + h) * 8 : (r * 2 + h + 1) * 8, j * 128 : (j + 1) * 128
                        ]

    def forward_y(n):
        for h in range(2):
            values = jnp.concatenate([zb[j, h * 128 : (h + 1) * 128, :] for j in range(4)], axis=1)
            result = table_dot(y_fwd, values, NT)
            gsend[n, h * 32 : (h + 1) * 32] = result.reshape(32, 8, 128)

    def forward_x(n, m):
        result = table_dot(x_fwd, grecv[n].reshape(512, 128))
        dsend[m] = result.reshape(DP, 32, 128)

    def inverse_x(m, n):
        result = table_dot(x_inv, drecv[m].reshape(128, 128))
        gsend[n] = result.reshape(GRID, 8, 128)

    need("z_fwd")
    for t in range(2):
        for c in range(2):
            load_snap(t, c, 6 + t * 2 + c).wait()
            forward_z(snap, lambda c: c * 4096 + t * 2048, z_fwd, c)
        if t == 0:
            need("y_fwd")
        forward_y(t)
        if t == 0:
            pl.semaphore_wait(barrier, GRID - 1 + DP - 1)
        grid_send(t, slot_of, place)

    def widen(i, _):
        rows = pl.ds(i * 512, 512)
        snap_f[rows, :] = snap[rows, :].astype(F32)
        return 0

    lax.fori_loop(0, 16, widen, 0)

    need("x_fwd")
    for t in range(2):
        grid_wait(t)
        forward_x(t, t)
        send_far(t)
        send_near(t)

    def w_tiles(r, c, t):
        return range(r * 16 + c * 8 + t * 4, r * 16 + c * 8 + t * 4 + 4)

    def w_read(ref, q, r, c, t):
        return jnp.concatenate([ref[pl.ds(j * 8 + q, 8, stride=256), :] for j in w_tiles(r, c, t)], axis=1)

    def w_write(ref, q, r, c, t, value):
        for n, j in enumerate(w_tiles(r, c, t)):
            ref[pl.ds(j * 8 + q, 8, stride=256), :] = value[:, n * 128 : (n + 1) * 128]

    def s_rows(t, s, c, r):
        return pl.ds(((t * 4 + s) * 2 + c) * 16 + r * 8, 8)

    def mix(t, side):
        high, low = split(drecv[t, pl.ds(side * 2, 2)].reshape(64, 128))

        def body(q, _):
            spectra = dot(high, spread[q]) + dot(low, spread[q])
            spec_x[q, pl.ds(pl.multiple_of(t * 128 + side * 64, 64), 64)] = spectra
            if t == 0:
                sums = [[jnp.zeros((8, 128), F32) for _ in range(2)] for _ in range(2)]
            else:
                sums = [[mixed[q, side * 2 + s, r * 8 : (r + 1) * 8, :] for r in range(2)] for s in range(2)]
            for c in range(2):
                w_re, w_im = w_read(weight, q, 0, c, t), w_read(weight, q, 1, c, t)
                for s in range(2):
                    row = (s * 2 + c) * 16
                    s_re, s_im = spectra[row : row + 8], spectra[row + 8 : row + 16]
                    products = (s_re * w_re - s_im * w_im, s_re * w_im + s_im * w_re)
                    for r in range(2):
                        for j in range(4):
                            sums[s][r] = sums[s][r] + products[r][:, j * 128 : (j + 1) * 128]
            for s in range(2):
                for r in range(2):
                    mixed[q, side * 2 + s, r * 8 : (r + 1) * 8, :] = sums[s][r]
            return 0

        lax.fori_loop(0, 8, body, 0, unroll=4)

    need("spread")
    need_state(0, weight)
    for t in range(2):
        wait_near(t)
        mix(t, near)
        wait_far(t)
        mix(t, far)
    need("gather")
    values = jnp.concatenate([mixed[q].reshape(64, 128) for q in range(8)], axis=1)
    result = dot_exact(values, gather[...])
    for c in range(2):
        dsend[2, :, c * 16 : (c + 1) * 16, :] = result[:, c * 128 : (c + 1) * 128].reshape(4, 16, 128)
    send_far(2)
    send_near(2)
    need("x_inv")
    wait_near(2)
    wait_far(2)

    inverse_x(2, 2)
    grid_send(2, place, slot_of)

    def strided(ref, cell, channels):
        return jnp.concatenate(
            [ref[pl.ds(cell * 4 + j, channels, stride=128), :] for j in range(4)], axis=1
        ).astype(BF16)

    def local_forward(i, _):
        result = dot(lw_t[...], strided(snap_f, i, C))
        for j in range(4):
            pre[pl.ds(i * 4 + j, CO, stride=128), :] = result[:, j * 128 : (j + 1) * 128]
        return 0

    need("lw")
    lax.fori_loop(0, 32, local_forward, 0, unroll=4)
    lw = lw_t[...].astype(F32).T.astype(BF16)
    need("y_inv", "z_inv_scaled", "cot")
    grid_wait(2)

    inverse_y(grecv.at[2], y_inv, ub)

    def through_gelu(rows, spectral):
        v = spectral + pre[rows, :]
        k = math.sqrt(2.0 / math.pi)
        square = v * v
        t = jnp.tanh(v * (k + (k * 0.044715) * square))
        bend = v * (0.5 * k + (1.5 * k * 0.044715) * square)
        slope = (0.5 + 0.5 * t) + bend * (1.0 - t * t)
        grad_b[rows, :] = (cot[rows, :].astype(F32) * slope).astype(BF16)

    need("z_fwd_scaled")
    for c in range(2):
        inverse_z(ub, z_inv_scaled, c, through_gelu)
        forward_z(grad_b, lambda c: c * 2048, z_fwd_scaled, c)
    forward_y(3)
    grid_send(3, slot_of, place)

    lsend[...] = jnp.zeros_like(lsend)

    def widen_grad(i, _):
        rows = pl.ds(i * 512, 512)
        grad_f[rows, :] = grad_b[rows, :].astype(F32)
        return 0

    lax.fori_loop(0, 8, widen_grad, 0)

    def local_grad(i, total):
        return total + dot(strided(grad_f, i, CO), strided(snap_f, i, C), NT)

    total = lax.fori_loop(0, 32, local_grad, jnp.zeros((CO, C), F32), unroll=4)
    gx, gz, gy = lax.div(me, 16), lax.rem(lax.div(me, 4), 4), lax.rem(me, 4)
    rounds = (
        (d, lambda j: {"dp": j}),
        (gy, lambda j: {"grid": me - gy + j}),
        (gz, lambda j: {"grid": me - 4 * gz + 4 * j}),
        (gx, lambda j: {"grid": me - 16 * gx + 16 * j}),
    )

    def local_send(n, value):
        mine, device = rounds[n]
        lsend[n, :, 0:C] = value

        def body(i, _):
            pltpu.make_async_remote_copy(
                src_ref=lsend.at[n],
                dst_ref=lrecv.at[n, mine],
                send_sem=lsend_sems.at[n],
                recv_sem=lrecv_sems.at[n],
                device_id=device(lax.rem(mine + i, 4)),
                device_id_type=MESH,
            ).start()
            return 0

        lax.fori_loop(1, 4, body, 0)
        lrecv[n, mine] = lsend[n]
        pending.append((lsend_sems, n, lrecv.at[n]))

    def local_sum(n):
        wait_all(lrecv_sems, n, lrecv.at[n])
        return ((lrecv[n, 0] + lrecv[n, 1]) + (lrecv[n, 2] + lrecv[n, 3]))[:, 0:C]

    local_send(0, total)

    def local_backward(i, _):
        result = dot(lw, strided(grad_f, i, CO))
        for j in range(4):
            for c in range(2):
                for t, ref in enumerate((back_a, back_b)):
                    row = c * 32 + t * 16
                    ref[pl.ds(c * 2048 + i * 4 + j, 16, stride=128), :] = result[
                        row : row + 16, j * 128 : (j + 1) * 128
                    ]
        return 0

    def store(n, src, dst):
        copy = pltpu.make_async_copy(src, dst, out_sems.at[n])
        copy.start()
        stored.append(copy)

    lax.fori_loop(0, 12, local_backward, 0, unroll=4)
    grid_wait(3)

    forward_x(3, 3)
    send_far(3)
    send_near(3)
    local_send(1, local_sum(0))

    def spread_gradients(side):
        rows = pl.ds(side * 2, 2)
        values = jnp.concatenate(
            [drecv[3, rows, c * 16 : (c + 1) * 16, :].reshape(32, 128) for c in range(2)], axis=1
        )
        result = dot_exact(values, gather[...], NT)
        for q in range(8):
            grad_x[q, rows] = result[:, q * 128 : (q + 1) * 128].reshape(2, 16, 128)

    def g_tile(q, s, r):
        return jnp.concatenate([grad_x[q, s, r * 8 : (r + 1) * 8, :]] * 4, axis=1)

    def input_modes(t, side):
        def body(q, total):
            parts = {}
            for c in range(2):
                w_re, w_im = w_read(weight, q, 0, c, t), w_read(weight, q, 1, c, t)
                for s in range(2):
                    g_re, g_im = g_tile(q, side * 2 + s, 0), g_tile(q, side * 2 + s, 1)
                    parts[s, c, 0] = w_re * g_re + w_im * g_im
                    parts[s, c, 1] = w_re * g_im - w_im * g_re
            values = jnp.concatenate(
                [parts[s, c, r] for s in range(2) for c in range(2) for r in range(2)], axis=0
            )
            return total + dot_exact(values, spread[q], NT)

        total = lax.fori_loop(0, 8, body, jnp.zeros((64, 128), F32), unroll=4)
        dsend[4 + t, pl.ds(side * 2, 2)] = total.reshape(2, 32, 128)

    wait_near(3)
    spread_gradients(near)
    for t in range(2):
        input_modes(t, near)
        send_near(4 + t)
    wait_far(3)
    spread_gradients(far)
    for t in range(2):
        input_modes(t, far)
        send_far(4 + t)
    local_send(2, local_sum(1))
    lax.fori_loop(12, 32, local_backward, 0, unroll=4)
    store(0, back_b, back_hbm)
    local_send(3, local_sum(2))

    need_state(1, first)
    need_state(2, second)

    def adam(q, _):
        for c in range(2):
            for t in range(2):
                re = im = None
                for s in range(4):
                    s_re = spec_x[q, s_rows(t, s, c, 0), :]
                    s_im = spec_x[q, s_rows(t, s, c, 1), :]
                    g_re, g_im = g_tile(q, s, 0), g_tile(q, s, 1)
                    a, b = s_re * g_re + s_im * g_im, s_re * g_im - s_im * g_re
                    re, im = (a, b) if re is None else (re + a, im + b)
                for r, g in enumerate((re, im)):
                    m = 0.9 * w_read(first, q, r, c, t) + 0.1 * g
                    v = 0.999 * w_read(second, q, r, c, t) + 0.001 * g * g
                    step = (m / (1.0 - 0.9**STEP)) / (jnp.sqrt(v / (1.0 - 0.999**STEP)) + 1e-8)
                    w_write(new_first, q, r, c, t, m)
                    w_write(new_second, q, r, c, t, v)
                    w_write(new_weight, q, r, c, t, w_read(weight, q, r, c, t) - RATE * step)
        return 0

    for t in range(2):
        wait_near(4 + t)
        wait_far(4 + t)
        inverse_x(4 + t, 4 + t)
        grid_send(4 + t, place, slot_of)
    lax.fori_loop(0, 8, adam, 0)
    states = ((new_weight, new_weight_hbm), (new_first, new_first_hbm), (new_second, new_second_hbm))

    for n, (src, dst) in enumerate(states):
        store(3 + n, src, dst)
    need("z_inv")
    grid_wait(4)
    inverse_y(grecv.at[4], y_inv, ub)

    def finish(rows, spectral):
        half[rows, :] = (spectral + back_a[rows, :]).astype(BF16)

    for c in range(2):
        inverse_z(ub, z_inv, c, finish)
    store(1, half, half_hbm)
    local_out[...] = local_sum(3)
    grid_wait(5)
    store(2, grecv.at[5], last_hbm)

    for sems, n, ref in pending:
        wait_all(sems, n, ref)
    for copy in stored:
        copy.wait()


def last_kernel(
    last_hbm, back_hbm, half_hbm, local, weight_hbm, first_hbm, second_hbm, y_inv_hbm, z_inv_hbm,
    out_hbm, local_out, new_weight_hbm, new_first_hbm, new_second_hbm,
    last, back, y_inv, z_inv, ub, half, half_a, weight, first, second, in_sems, out_sems,
):
    sources = (last_hbm, y_inv_hbm, z_inv_hbm, back_hbm, half_hbm, weight_hbm, first_hbm, second_hbm)
    places = (last, y_inv, z_inv, back, half_a, weight, first, second)
    loads = [pltpu.make_async_copy(a, b, in_sems.at[n]) for n, (a, b) in enumerate(zip(sources, places))]
    for copy in loads:
        copy.start()
    stores = []

    def store(src, dst):
        copy = pltpu.make_async_copy(src, dst, out_sems.at[len(stores)])
        copy.start()
        stores.append(copy)

    def finish(rows, spectral):
        half[rows, :] = (spectral + back[rows, :]).astype(BF16)

    def store_half(src, t, c):
        store(src.at[pl.ds(c * 2048, 2048)], out_hbm.at[pl.ds(c * 4096 + t * 2048, 2048)])

    local_out[...] = local[...]
    loads[0].wait()
    loads[1].wait()
    inverse_y(last, y_inv, ub)
    loads[2].wait()
    loads[3].wait()
    inverse_z(ub, z_inv, 0, finish)
    store_half(half, 1, 0)
    loads[4].wait()
    for c in range(2):
        store_half(half_a, 0, c)
    for copy, src, dst in zip(loads[5:], places[5:], (new_weight_hbm, new_first_hbm, new_second_hbm)):
        copy.wait()
        store(src, dst)
    inverse_z(ub, z_inv, 1, finish)
    store_half(half, 1, 1)
    for copy in stores:
        copy.wait()


def to_rows(state):
    return state.reshape(8, 8, 32, 128).transpose(0, 2, 1, 3).reshape(2048, 128)


def from_rows(rows):
    return rows.reshape(8, 32, 8, 128).transpose(0, 2, 1, 3).reshape(8, 8, 4096)


def on_device(tables, snapshots, cotangent, local_weight, spectral_weight, first_moment, second_moment):
    vmem = pl.BlockSpec(memory_space=pltpu.VMEM)
    hbm = pl.BlockSpec(memory_space=pl.ANY)
    shape = jax.ShapeDtypeStruct
    state = shape((2048, 128), F32)
    state_scratch = pltpu.VMEM((2048, 128), F32)
    sems = lambda n: pltpu.SemaphoreType.DMA((n,))
    table_scratch = [pltpu.VMEM(table.shape, BF16) for table in tables]
    params = lambda **more: pltpu.CompilerParams(
        has_side_effects=True, vmem_limit_bytes=56 * 1024 * 1024, **more
    )
    last, back, half, local_grad, new_weight, new_first, new_second = pl.pallas_call(
        kernel,
        out_shape=(
            shape((GRID, 8, 128), F32), shape((4096, 128), F32), shape((4096, 128), BF16), shape((CO, C), F32),
            state, state, state,
        ),
        in_specs=[hbm] * (6 + len(tables)),
        out_specs=(hbm,) * 3 + (vmem,) + (hbm,) * 3,
        scratch_shapes=[
            pltpu.VMEM((8192, 128), BF16),
            pltpu.VMEM((4096, 128), BF16),
            pltpu.VMEM((CO, C), BF16),
        ]
        + table_scratch
        + [state_scratch] * 6
        + [
            pltpu.VMEM((4, 256, 128), F32),
            pltpu.VMEM((8192, 128), F32),
            pltpu.VMEM((4096, 128), F32),
            pltpu.VMEM((4096, 128), F32),
            pltpu.VMEM((4096, 128), F32),
            pltpu.VMEM((4096, 128), BF16),
            pltpu.VMEM((4096, 128), F32),
            pltpu.VMEM((4, 256, 128), F32),
            pltpu.VMEM((8, 256, 512), F32),
            pltpu.VMEM((8, 4, 16, 128), F32),
            pltpu.VMEM((8, 4, 16, 128), F32),
            pltpu.VMEM((4096, 128), BF16),
            pltpu.VMEM((6, GRID, 8, 128), F32),
            pltpu.VMEM((6, GRID, 8, 128), F32),
            pltpu.VMEM((6, DP, 32, 128), F32),
            pltpu.VMEM((6, DP, 32, 128), F32),
            pltpu.VMEM((4, CO, 128), F32),
            pltpu.VMEM((4, 4, CO, 128), F32),
        ]
        + [sems(n) for n in (16, 10, 6, 6, 6, 12, 12, 4, 4)],
        compiler_params=params(collective_id=0),
    )(
        snapshots.reshape(8192, 128),
        cotangent.reshape(4096, 128),
        local_weight.T,
        to_rows(spectral_weight),
        to_rows(first_moment),
        to_rows(second_moment),
        *tables,
    )
    named = dict(zip(TABLES, tables))
    grad_input, local_grad, new_weight, new_first, new_second = pl.pallas_call(
        last_kernel,
        out_shape=(shape((8192, 128), BF16), shape((CO, C), F32), state, state, state),
        in_specs=[hbm] * 3 + [vmem] + [hbm] * 5,
        out_specs=(hbm, vmem) + (hbm,) * 3,
        scratch_shapes=[
            pltpu.VMEM((GRID, 8, 128), F32),
            pltpu.VMEM((4096, 128), F32),
            pltpu.VMEM(named["y_inv"].shape, BF16),
            pltpu.VMEM(named["z_inv"].shape, BF16),
            pltpu.VMEM((4, 256, 128), F32),
            pltpu.VMEM((4096, 128), BF16),
            pltpu.VMEM((4096, 128), BF16),
        ]
        + [state_scratch] * 3
        + [sems(8), sems(7)],
        compiler_params=params(),
    )(last, back, half, local_grad, new_weight, new_first, new_second, named["y_inv"], named["z_inv"])
    return (
        grad_input.reshape(snapshots.shape),
        local_grad.T,
        from_rows(new_weight),
        from_rows(new_first),
        from_rows(new_second),
    )


def solution(mesh):
    tables = make_tables()
    split_spec = P("dp", "grid", None)
    field_spec = P("dp", None, "grid", None, None)

    def step(*args):
        return on_device(tables, *args)

    return jax.shard_map(
        step,
        mesh=mesh,
        in_specs=(field_spec, field_spec, P(), split_spec, split_spec, split_spec),
        out_specs=(field_spec, P(), split_spec, split_spec, split_spec),
        check_vma=False,
    )
```

```python
import math

import jax
import jax.numpy as jnp
import ml_dtypes
import numpy as np
from jax import lax
from jax.experimental import pallas as pl
from jax.experimental.pallas import tpu as pltpu
from jax.sharding import PartitionSpec as P

NX = 128
NY = 64
NZ = 128
KX = 32
KY = 32
KZ = 16
STEP = 100
C = 64
CO = 32
GRID = 64
DP = 4
RATE = 0.02

MESH = pl.DeviceIdType.MESH
F32 = jnp.float32
BF16 = jnp.bfloat16
NN = (((1,), (0,)), ((), ()))
NT = (((1,), (1,)), ((), ()))


def mode_numbers(length, retained):
    a = np.arange(retained)
    return np.where(a < retained // 2, a, length - retained + a)


def angles(length, numbers):
    points = np.arange(length)
    return (points[:, None] * numbers[None, :] % length) * (2.0 * math.pi / length)


def rotation(theta, direction):
    cos, sin = np.cos(theta), direction * np.sin(theta)
    return np.stack([np.stack([cos, sin]), np.stack([-sin, cos])])


def split_table(table):
    high = table.astype(ml_dtypes.bfloat16)
    low = (table - high.astype(np.float64)).astype(ml_dtypes.bfloat16)
    return np.stack([high, low])


def make_tables():
    z_angles = angles(NZ, np.arange(KZ))
    fold = np.where(np.arange(KZ) == 0, 1.0, 2.0) / (NX * NY * NZ)
    z_fwd = np.concatenate([np.cos(z_angles).T, -np.sin(z_angles).T]).astype(ml_dtypes.bfloat16)
    z_fwd_scaled = (z_fwd.astype(np.float64) * np.tile(fold, 2)[:, None]).astype(ml_dtypes.bfloat16)
    z_inv = np.concatenate([np.cos(z_angles).T, -np.sin(z_angles).T])
    z_inv_scaled = z_inv * np.tile(fold, 2)[:, None]

    def four(table):
        out = np.zeros((4, 2 * KZ, 4, NZ))
        for j in range(4):
            out[j, :, j] = table
        return split_table(out.reshape(4 * 2 * KZ, 4 * NZ))

    y_theta = angles(NY, mode_numbers(NY, KY))
    x_theta = angles(NX, mode_numbers(NX, KX))
    y_rot = rotation(y_theta, -1.0)
    x_rot = rotation(x_theta, -1.0)
    x_rot = x_rot.reshape(2, 2, GRID, 2, DP, KX // DP)
    yi_rot = rotation(y_theta.T, 1.0)
    xi_rot = rotation(x_theta.T, 1.0)
    xi_rot = xi_rot.reshape(2, 2, DP, KX // DP, GRID, 2)
    y_fwd = np.zeros((KY, 2, 2, 2, 2, 2, 2, NY))
    x_fwd = np.zeros((DP, 2, 2, 8, GRID, 2, 2, 2))
    x_inv = np.zeros((GRID, 2, 2, 2, DP, 2, 2, 8))
    y_inv = np.zeros((KY, 2, 2, 2, 2, 2, 2, NY))
    for c in range(2):
        x_fwd[:, c, :, :, :, c] = x_rot.transpose(4, 1, 5, 2, 3, 0)
        x_inv[:, c, :, :, :, c] = xi_rot.transpose(4, 5, 1, 2, 0, 3)
        for x in range(2):
            y_fwd[:, c, x, :, c, :, x] = y_rot.transpose(3, 1, 0, 2)
            y_inv[:, c, x, :, c, :, x] = yi_rot.transpose(2, 0, 1, 3)
    spread = np.zeros((8, 16, 8, 16, 32))
    for q in range(8):
        for c in range(16):
            spread[q, c, q, c] = 1.0
    gather = np.zeros((8, 4, 32, 32, 8))
    for q in range(8):
        for o in range(32):
            gather[q, :, o, o, q] = 1.0
    return (
        z_fwd,
        z_fwd_scaled,
        four(z_inv_scaled),
        four(z_inv),
        split_table(y_fwd.reshape(256, 512)),
        split_table(x_fwd.reshape(128, 512)),
        split_table(x_inv.reshape(512, 128)),
        split_table(y_inv.reshape(256, 512)),
        spread.reshape(8, 128, 512).astype(ml_dtypes.bfloat16),
        gather.reshape(1024, 256).astype(ml_dtypes.bfloat16),
    )


def dot(a, b, dims=NN):
    return lax.dot_general(a, b, dims, preferred_element_type=F32)


def split(a):
    high = a.astype(BF16)
    return high, (a - high.astype(F32)).astype(BF16)


def table_dot(table, values, dims=NN):
    high, low = split(values)
    return dot(table[0], high, dims) + dot(table[0], low, dims) + dot(table[1], high, dims)


def dot_table(values, table):
    high, low = split(values)
    return dot(high, table[0]) + dot(low, table[0]) + dot(high, table[1])


def dot_exact(values, table, dims=NN):
    high, low = split(values)
    return dot(high, table, dims) + dot(low, table, dims)


def dp_and_grid():
    return lax.axis_index("dp"), lax.axis_index("grid")


def inverse_y(recv, table, ub):
    for h in range(2):
        values = recv[h * 32 : (h + 1) * 32].reshape(256, 128).T
        result = dot_table(values, table)
        for j in range(4):
            ub[j, h * 128 : (h + 1) * 128, :] = result[:, j * 128 : (j + 1) * 128]


def inverse_z(ub, table, c, finish):
    def body(i, _):
        groups = []
        for g in range(2):
            row = i * 64 + g * 32
            parts = [
                ub[c * 2 + s, pl.ds(row + h * 128 + j * 8, 8), :]
                for j in range(4) for s in range(2) for h in range(2)
            ]
            groups.append(jnp.concatenate(parts, axis=0).T)
        high, low = split(jnp.concatenate(groups, axis=0))
        tables = jnp.concatenate([table[0], table[0], table[1]], axis=0)
        result = dot(jnp.concatenate([high, low, high], axis=1), tables)
        for g in range(2):
            for j in range(4):
                finish(
                    pl.ds(c * 2048 + i * 1024 + g * 512 + j * 128, 128),
                    result[g * 128 : (g + 1) * 128, j * 128 : (j + 1) * 128],
                )
        return 0

    lax.fori_loop(0, 2, body, 0, unroll=2)


TABLES = (
    "z_fwd", "z_fwd_scaled", "z_inv_scaled", "z_inv", "y_fwd", "x_fwd", "x_inv", "y_inv", "spread", "gather"
)


def kernel(
    snap_hbm, cot_hbm, lw_hbm, weight_hbm, first_hbm, second_hbm,
    z_fwd_hbm, z_fwd_scaled_hbm, z_inv_scaled_hbm, z_inv_hbm, y_fwd_hbm, x_fwd_hbm, x_inv_hbm, y_inv_hbm,
    spread_hbm, gather_hbm,
    last_hbm, back_hbm, half_hbm, local_out, new_weight_hbm, new_first_hbm, new_second_hbm,
    snap, cot, lw_t, z_fwd, z_fwd_scaled, z_inv_scaled, z_inv, y_fwd, x_fwd, x_inv, y_inv, spread, gather,
    weight, first, second, new_weight, new_first, new_second,
    zb, snap_f, pre, back_a, back_b, grad_b, grad_f, ub, spec_x, mixed, grad_x, half,
    gsend, grecv, dsend, drecv, lsend, lrecv,
    load_sems, state_sems, out_sems, gsend_sems, grecv_sems, dsend_sems, drecv_sems, lsend_sems, lrecv_sems,
):
    d, me = dp_and_grid()
    slot_of = lambda g: lax.rem(g, 2) * 32 + lax.div(g, 2)
    place = lambda g: g
    pending, stored = [], []

    barrier = pltpu.get_barrier_semaphore()

    def greet_grid(i, _):
        pl.semaphore_signal(barrier, inc=1, device_id={"grid": lax.rem(me + i, GRID)}, device_id_type=MESH)
        return 0

    def greet_dp(i, _):
        pl.semaphore_signal(barrier, inc=1, device_id={"dp": lax.rem(d + i, DP)}, device_id_type=MESH)
        return 0

    lax.fori_loop(1, DP, greet_dp, 0)

    loads = {}

    def load(name, src, dst):
        copy = pltpu.make_async_copy(src, dst, load_sems.at[len(loads)])
        copy.start()
        loads[name] = copy

    def need(*names):
        for name in names:
            loads.pop(name).wait()

    def snap_rows(t, c):
        return pl.ds(c * 4096 + t * 2048, 2048)

    def load_snap(t, c, n):
        rows = snap_rows(t, c)
        return pltpu.make_async_copy(snap_hbm.at[rows], snap.at[rows], state_sems.at[n])

    load("z_fwd", z_fwd_hbm, z_fwd)
    load_snap(0, 0, 6).start()
    load_snap(0, 1, 7).start()
    load("y_fwd", y_fwd_hbm, y_fwd)
    load_snap(1, 0, 8).start()
    load_snap(1, 1, 9).start()

    lax.fori_loop(1, GRID, greet_grid, 0)

    load("x_fwd", x_fwd_hbm, x_fwd)
    load("spread", spread_hbm, spread)

    def load_state(n, src, dst):
        pltpu.make_async_copy(src, dst, state_sems.at[n]).start()

    def need_state(n, dst):
        pltpu.make_async_copy(dst, dst, state_sems.at[n]).wait()

    load_state(0, weight_hbm, weight)
    load("gather", gather_hbm, gather)
    load("lw", lw_hbm, lw_t)
    load("x_inv", x_inv_hbm, x_inv)
    load("y_inv", y_inv_hbm, y_inv)
    load("z_inv_scaled", z_inv_scaled_hbm, z_inv_scaled)
    load("cot", cot_hbm, cot)
    load("z_fwd_scaled", z_fwd_scaled_hbm, z_fwd_scaled)
    load_state(1, first_hbm, first)
    load_state(2, second_hbm, second)
    load("z_inv", z_inv_hbm, z_inv)

    def grid_send(n, src_slot, dst_slot):
        def body(i, _):
            to = lax.rem(me + i, GRID)
            pltpu.make_async_remote_copy(
                src_ref=gsend.at[n, src_slot(to)],
                dst_ref=grecv.at[n, dst_slot(me)],
                send_sem=gsend_sems.at[n],
                recv_sem=grecv_sems.at[n],
                device_id={"grid": to},
                device_id_type=MESH,
            ).start()
            return 0

        lax.fori_loop(1, GRID, body, 0)
        grecv[n, dst_slot(me)] = gsend[n, src_slot(me)]
        pending.append((gsend_sems, n, gsend.at[n]))

    near = lax.div(d, 2)
    far = 1 - near
    core = lax.rem(d, 2)

    def dp_copy(n, sem, to):
        pltpu.make_async_remote_copy(
            src_ref=dsend.at[n, to],
            dst_ref=drecv.at[n, d],
            send_sem=dsend_sems.at[sem],
            recv_sem=drecv_sems.at[sem],
            device_id={"dp": to},
            device_id_type=MESH,
        ).start()

    def send_far(n):
        for i in range(2):
            dp_copy(n, n, far * 2 + lax.rem(core + i, 2))
        pending.append((dsend_sems, n, dsend.at[n, pl.ds(0, 3)]))

    def send_near(n):
        dp_copy(n, 6 + n, near * 2 + 1 - core)
        drecv[n, d] = dsend[n, d]
        pending.append((dsend_sems, 6 + n, dsend.at[n, pl.ds(0, 2)]))

    def wait_all(sems, n, ref):
        part = ref.at[pl.ds(0, ref.shape[0] - 1)]
        pltpu.make_async_copy(part, part, sems.at[n]).wait()

    def grid_wait(n):
        wait_all(grecv_sems, n, grecv.at[n])

    def wait_far(n):
        wait_all(drecv_sems, n, drecv.at[n, pl.ds(0, 3)])

    def wait_near(n):
        wait_all(drecv_sems, 6 + n, drecv.at[n, pl.ds(0, 2)])

    def forward_z(field, row_of, table, c):
        for part in range(2):
            start = row_of(c) + part * 1024
            z = dot(table[...], field[pl.ds(start, 1024), :], NT)
            for r in range(2):
                for h in range(2):
                    for j in range(8):
                        row = h * 128 + (part * 8 + j) * 8
                        zb[c * 2 + r, row : row + 8, :] = z[
                            (r * 2 + h) * 8 : (r * 2 + h + 1) * 8, j * 128 : (j + 1) * 128
                        ]

    def forward_y(n):
        for h in range(2):
            values = jnp.concatenate([zb[j, h * 128 : (h + 1) * 128, :] for j in range(4)], axis=1)
            result = table_dot(y_fwd, values, NT)
            gsend[n, h * 32 : (h + 1) * 32] = result.reshape(32, 8, 128)

    def forward_x(n, m):
        result = table_dot(x_fwd, grecv[n].reshape(512, 128))
        dsend[m] = result.reshape(DP, 32, 128)

    def inverse_x(m, n):
        high, low = split(drecv[m].reshape(128, 128))
        tables = jnp.concatenate([x_inv[0], x_inv[0], x_inv[1]], axis=1)
        result = dot(tables, jnp.concatenate([high, low, high], axis=0))
        gsend[n] = result.reshape(GRID, 8, 128)

    need("z_fwd")
    for t in range(2):
        for c in range(2):
            load_snap(t, c, 6 + t * 2 + c).wait()
            forward_z(snap, lambda c: c * 4096 + t * 2048, z_fwd, c)
        if t == 0:
            need("y_fwd")
        forward_y(t)
        if t == 0:
            pl.semaphore_wait(barrier, GRID - 1 + DP - 1)
        grid_send(t, slot_of, place)

    def widen(i, _):
        rows = pl.ds(i * 512, 512)
        snap_f[rows, :] = snap[rows, :].astype(F32)
        return 0

    lax.fori_loop(0, 16, widen, 0)

    need("x_fwd")
    for t in range(2):
        grid_wait(t)
        forward_x(t, t)
        send_far(t)
        send_near(t)

    def w_tiles(r, c, t):
        return range(r * 16 + c * 8 + t * 4, r * 16 + c * 8 + t * 4 + 4)

    def w_read(ref, q, r, c, t):
        return jnp.concatenate([ref[pl.ds(j * 8 + q, 8, stride=256), :] for j in w_tiles(r, c, t)], axis=1)

    def w_write(ref, q, r, c, t, value):
        for n, j in enumerate(w_tiles(r, c, t)):
            ref[pl.ds(j * 8 + q, 8, stride=256), :] = value[:, n * 128 : (n + 1) * 128]

    def s_rows(t, s, c, r):
        return pl.ds(((t * 4 + s) * 2 + c) * 16 + r * 8, 8)

    def mix(t, side):
        halves = jnp.concatenate(split(drecv[t, pl.ds(side * 2, 2)].reshape(64, 128)), axis=1)

        def body(q, _):
            spectra = dot(halves, jnp.concatenate([spread[q], spread[q]], axis=0))
            spec_x[q, pl.ds(pl.multiple_of(t * 128 + side * 64, 64), 64)] = spectra
            if t == 0:
                sums = [[jnp.zeros((8, 128), F32) for _ in range(2)] for _ in range(2)]
            else:
                sums = [[mixed[q, side * 2 + s, r * 8 : (r + 1) * 8, :] for r in range(2)] for s in range(2)]
            for c in range(2):
                w_re, w_im = w_read(weight, q, 0, c, t), w_read(weight, q, 1, c, t)
                for s in range(2):
                    row = (s * 2 + c) * 16
                    s_re, s_im = spectra[row : row + 8], spectra[row + 8 : row + 16]
                    products = (s_re * w_re - s_im * w_im, s_re * w_im + s_im * w_re)
                    for r in range(2):
                        for j in range(4):
                            sums[s][r] = sums[s][r] + products[r][:, j * 128 : (j + 1) * 128]
            for s in range(2):
                for r in range(2):
                    mixed[q, side * 2 + s, r * 8 : (r + 1) * 8, :] = sums[s][r]
            return 0

        lax.fori_loop(0, 8, body, 0, unroll=4)

    need("spread")
    need_state(0, weight)
    for t in range(2):
        wait_near(t)
        mix(t, near)
        wait_far(t)
        mix(t, far)
    need("gather")
    values = jnp.concatenate([mixed[q].reshape(64, 128) for q in range(8)], axis=1)
    result = dot_exact(values, gather[...])
    for c in range(2):
        dsend[2, :, c * 16 : (c + 1) * 16, :] = result[:, c * 128 : (c + 1) * 128].reshape(4, 16, 128)
    send_far(2)
    send_near(2)
    need("x_inv")
    wait_near(2)
    wait_far(2)

    inverse_x(2, 2)
    grid_send(2, place, slot_of)

    def strided(ref, cell, channels):
        return jnp.concatenate(
            [ref[pl.ds(cell * 4 + j, channels, stride=128), :] for j in range(4)], axis=1
        ).astype(BF16)

    def local_forward(i, _):
        result = dot(lw_t[...], strided(snap_f, i, C))
        for j in range(4):
            pre[pl.ds(i * 4 + j, CO, stride=128), :] = result[:, j * 128 : (j + 1) * 128]
        return 0

    need("lw")
    lax.fori_loop(0, 32, local_forward, 0, unroll=4)
    lw = lw_t[...].astype(F32).T.astype(BF16)
    need("y_inv", "z_inv_scaled", "cot")
    grid_wait(2)

    inverse_y(grecv.at[2], y_inv, ub)

    def through_gelu(rows, spectral):
        v = spectral + pre[rows, :]
        k = math.sqrt(2.0 / math.pi)
        square = v * v
        t = jnp.tanh(v * (k + (k * 0.044715) * square))
        bend = v * (0.5 * k + (1.5 * k * 0.044715) * square)
        slope = (0.5 + 0.5 * t) + bend * (1.0 - t * t)
        grad_b[rows, :] = (cot[rows, :].astype(F32) * slope).astype(BF16)

    need("z_fwd_scaled")
    for c in range(2):
        inverse_z(ub, z_inv_scaled, c, through_gelu)
        forward_z(grad_b, lambda c: c * 2048, z_fwd_scaled, c)
    forward_y(3)
    grid_send(3, slot_of, place)

    lsend[...] = jnp.zeros_like(lsend)

    def widen_grad(i, _):
        rows = pl.ds(i * 512, 512)
        grad_f[rows, :] = grad_b[rows, :].astype(F32)
        return 0

    lax.fori_loop(0, 8, widen_grad, 0)

    def local_grad(i, total):
        return total + dot(strided(grad_f, i, CO), strided(snap_f, i, C), NT)

    total = lax.fori_loop(0, 32, local_grad, jnp.zeros((CO, C), F32), unroll=4)
    gx, gz, gy = lax.div(me, 16), lax.rem(lax.div(me, 4), 4), lax.rem(me, 4)
    rounds = (
        (d, lambda j: {"dp": j}),
        (gy, lambda j: {"grid": me - gy + j}),
        (gz, lambda j: {"grid": me - 4 * gz + 4 * j}),
        (gx, lambda j: {"grid": me - 16 * gx + 16 * j}),
    )

    def local_send(n, value):
        mine, device = rounds[n]
        lsend[n, :, 0:C] = value

        def body(i, _):
            pltpu.make_async_remote_copy(
                src_ref=lsend.at[n],
                dst_ref=lrecv.at[n, mine],
                send_sem=lsend_sems.at[n],
                recv_sem=lrecv_sems.at[n],
                device_id=device(lax.rem(mine + i, 4)),
                device_id_type=MESH,
            ).start()
            return 0

        lax.fori_loop(1, 4, body, 0)
        lrecv[n, mine] = lsend[n]
        pending.append((lsend_sems, n, lrecv.at[n]))

    def local_sum(n):
        wait_all(lrecv_sems, n, lrecv.at[n])
        return ((lrecv[n, 0] + lrecv[n, 1]) + (lrecv[n, 2] + lrecv[n, 3]))[:, 0:C]

    local_send(0, total)

    def local_backward(i, _):
        result = dot(lw, strided(grad_f, i, CO))
        for j in range(4):
            for c in range(2):
                for t, ref in enumerate((back_a, back_b)):
                    row = c * 32 + t * 16
                    ref[pl.ds(c * 2048 + i * 4 + j, 16, stride=128), :] = result[
                        row : row + 16, j * 128 : (j + 1) * 128
                    ]
        return 0

    def store(n, src, dst):
        copy = pltpu.make_async_copy(src, dst, out_sems.at[n])
        copy.start()
        stored.append(copy)

    lax.fori_loop(0, 12, local_backward, 0, unroll=4)
    grid_wait(3)

    forward_x(3, 3)
    send_far(3)
    send_near(3)
    local_send(1, local_sum(0))

    def spread_gradients(side):
        rows = pl.ds(side * 2, 2)
        values = jnp.concatenate(
            [drecv[3, rows, c * 16 : (c + 1) * 16, :].reshape(32, 128) for c in range(2)], axis=1
        )
        result = dot_exact(values, gather[...], NT)
        for q in range(8):
            grad_x[q, rows] = result[:, q * 128 : (q + 1) * 128].reshape(2, 16, 128)

    def g_tile(q, s, r):
        return jnp.concatenate([grad_x[q, s, r * 8 : (r + 1) * 8, :]] * 4, axis=1)

    def input_modes(t, side):
        def body(q, total):
            parts = {}
            for c in range(2):
                w_re, w_im = w_read(weight, q, 0, c, t), w_read(weight, q, 1, c, t)
                for s in range(2):
                    g_re, g_im = g_tile(q, side * 2 + s, 0), g_tile(q, side * 2 + s, 1)
                    parts[s, c, 0] = w_re * g_re + w_im * g_im
                    parts[s, c, 1] = w_re * g_im - w_im * g_re
            values = jnp.concatenate(
                [parts[s, c, r] for s in range(2) for c in range(2) for r in range(2)], axis=0
            )
            return total + dot_exact(values, spread[q], NT)

        total = lax.fori_loop(0, 8, body, jnp.zeros((64, 128), F32), unroll=4)
        dsend[4 + t, pl.ds(side * 2, 2)] = total.reshape(2, 32, 128)

    wait_near(3)
    spread_gradients(near)
    for t in range(2):
        input_modes(t, near)
        send_near(4 + t)
    wait_far(3)
    spread_gradients(far)
    for t in range(2):
        input_modes(t, far)
        send_far(4 + t)
    local_send(2, local_sum(1))
    lax.fori_loop(12, 32, local_backward, 0, unroll=4)
    store(0, back_b, back_hbm)
    local_send(3, local_sum(2))

    need_state(1, first)
    need_state(2, second)

    def adam(q, _):
        for c in range(2):
            for t in range(2):
                re = im = None
                for s in range(4):
                    s_re = spec_x[q, s_rows(t, s, c, 0), :]
                    s_im = spec_x[q, s_rows(t, s, c, 1), :]
                    g_re, g_im = g_tile(q, s, 0), g_tile(q, s, 1)
                    a, b = s_re * g_re + s_im * g_im, s_re * g_im - s_im * g_re
                    re, im = (a, b) if re is None else (re + a, im + b)
                for r, g in enumerate((re, im)):
                    m = 0.9 * w_read(first, q, r, c, t) + 0.1 * g
                    v = 0.999 * w_read(second, q, r, c, t) + 0.001 * g * g
                    step = (m / (1.0 - 0.9**STEP)) / (jnp.sqrt(v / (1.0 - 0.999**STEP)) + 1e-8)
                    w_write(new_first, q, r, c, t, m)
                    w_write(new_second, q, r, c, t, v)
                    w_write(new_weight, q, r, c, t, w_read(weight, q, r, c, t) - RATE * step)
        return 0

    for t in range(2):
        wait_near(4 + t)
        wait_far(4 + t)
        inverse_x(4 + t, 4 + t)
        grid_send(4 + t, place, slot_of)
    lax.fori_loop(0, 8, adam, 0)
    states = ((new_weight, new_weight_hbm), (new_first, new_first_hbm), (new_second, new_second_hbm))

    for n, (src, dst) in enumerate(states):
        store(3 + n, src, dst)
    need("z_inv")
    grid_wait(4)
    inverse_y(grecv.at[4], y_inv, ub)

    def finish(rows, spectral):
        half[rows, :] = (spectral + back_a[rows, :]).astype(BF16)

    for c in range(2):
        inverse_z(ub, z_inv, c, finish)
    store(1, half, half_hbm)
    local_out[...] = local_sum(3)
    grid_wait(5)
    store(2, grecv.at[5], last_hbm)

    for sems, n, ref in pending:
        wait_all(sems, n, ref)
    for copy in stored:
        copy.wait()


def last_kernel(
    last_hbm, back_hbm, half_hbm, local, weight_hbm, first_hbm, second_hbm, y_inv_hbm, z_inv_hbm,
    out_hbm, local_out, new_weight_hbm, new_first_hbm, new_second_hbm,
    last, back, y_inv, z_inv, ub, half, half_a, weight, first, second, in_sems, out_sems,
):
    sources = (last_hbm, y_inv_hbm, z_inv_hbm, back_hbm, half_hbm, weight_hbm, first_hbm, second_hbm)
    places = (last, y_inv, z_inv, back, half_a, weight, first, second)
    loads = [pltpu.make_async_copy(a, b, in_sems.at[n]) for n, (a, b) in enumerate(zip(sources, places))]
    for copy in loads:
        copy.start()
    stores = []

    def store(src, dst):
        copy = pltpu.make_async_copy(src, dst, out_sems.at[len(stores)])
        copy.start()
        stores.append(copy)

    def finish(rows, spectral):
        half[rows, :] = (spectral + back[rows, :]).astype(BF16)

    def store_half(src, t, c):
        store(src.at[pl.ds(c * 2048, 2048)], out_hbm.at[pl.ds(c * 4096 + t * 2048, 2048)])

    local_out[...] = local[...]
    loads[0].wait()
    loads[1].wait()
    inverse_y(last, y_inv, ub)
    loads[2].wait()
    loads[3].wait()
    inverse_z(ub, z_inv, 0, finish)
    store_half(half, 1, 0)
    loads[4].wait()
    for c in range(2):
        store_half(half_a, 0, c)
    for copy, src, dst in zip(loads[5:], places[5:], (new_weight_hbm, new_first_hbm, new_second_hbm)):
        copy.wait()
        store(src, dst)
    inverse_z(ub, z_inv, 1, finish)
    store_half(half, 1, 1)
    for copy in stores:
        copy.wait()


def to_rows(state):
    return state.reshape(8, 8, 32, 128).transpose(0, 2, 1, 3).reshape(2048, 128)


def from_rows(rows):
    return rows.reshape(8, 32, 8, 128).transpose(0, 2, 1, 3).reshape(8, 8, 4096)


def on_device(tables, snapshots, cotangent, local_weight, spectral_weight, first_moment, second_moment):
    vmem = pl.BlockSpec(memory_space=pltpu.VMEM)
    hbm = pl.BlockSpec(memory_space=pl.ANY)
    shape = jax.ShapeDtypeStruct
    state = shape((2048, 128), F32)
    state_scratch = pltpu.VMEM((2048, 128), F32)
    sems = lambda n: pltpu.SemaphoreType.DMA((n,))
    table_scratch = [pltpu.VMEM(table.shape, BF16) for table in tables]
    params = lambda **more: pltpu.CompilerParams(
        has_side_effects=True, vmem_limit_bytes=56 * 1024 * 1024, **more
    )
    last, back, half, local_grad, new_weight, new_first, new_second = pl.pallas_call(
        kernel,
        out_shape=(
            shape((GRID, 8, 128), F32), shape((4096, 128), F32), shape((4096, 128), BF16), shape((CO, C), F32),
            state, state, state,
        ),
        in_specs=[hbm] * (6 + len(tables)),
        out_specs=(hbm,) * 3 + (vmem,) + (hbm,) * 3,
        scratch_shapes=[
            pltpu.VMEM((8192, 128), BF16),
            pltpu.VMEM((4096, 128), BF16),
            pltpu.VMEM((CO, C), BF16),
        ]
        + table_scratch
        + [state_scratch] * 6
        + [
            pltpu.VMEM((4, 256, 128), F32),
            pltpu.VMEM((8192, 128), F32),
            pltpu.VMEM((4096, 128), F32),
            pltpu.VMEM((4096, 128), F32),
            pltpu.VMEM((4096, 128), F32),
            pltpu.VMEM((4096, 128), BF16),
            pltpu.VMEM((4096, 128), F32),
            pltpu.VMEM((4, 256, 128), F32),
            pltpu.VMEM((8, 256, 512), F32),
            pltpu.VMEM((8, 4, 16, 128), F32),
            pltpu.VMEM((8, 4, 16, 128), F32),
            pltpu.VMEM((4096, 128), BF16),
            pltpu.VMEM((6, GRID, 8, 128), F32),
            pltpu.VMEM((6, GRID, 8, 128), F32),
            pltpu.VMEM((6, DP, 32, 128), F32),
            pltpu.VMEM((6, DP, 32, 128), F32),
            pltpu.VMEM((4, CO, 128), F32),
            pltpu.VMEM((4, 4, CO, 128), F32),
        ]
        + [sems(n) for n in (16, 10, 6, 6, 6, 12, 12, 4, 4)],
        compiler_params=params(collective_id=0),
    )(
        snapshots.reshape(8192, 128),
        cotangent.reshape(4096, 128),
        local_weight.T,
        to_rows(spectral_weight),
        to_rows(first_moment),
        to_rows(second_moment),
        *tables,
    )
    named = dict(zip(TABLES, tables))
    grad_input, local_grad, new_weight, new_first, new_second = pl.pallas_call(
        last_kernel,
        out_shape=(shape((8192, 128), BF16), shape((CO, C), F32), state, state, state),
        in_specs=[hbm] * 3 + [vmem] + [hbm] * 5,
        out_specs=(hbm, vmem) + (hbm,) * 3,
        scratch_shapes=[
            pltpu.VMEM((GRID, 8, 128), F32),
            pltpu.VMEM((4096, 128), F32),
            pltpu.VMEM(named["y_inv"].shape, BF16),
            pltpu.VMEM(named["z_inv"].shape, BF16),
            pltpu.VMEM((4, 256, 128), F32),
            pltpu.VMEM((4096, 128), BF16),
            pltpu.VMEM((4096, 128), BF16),
        ]
        + [state_scratch] * 3
        + [sems(8), sems(7)],
        compiler_params=params(),
    )(last, back, half, local_grad, new_weight, new_first, new_second, named["y_inv"], named["z_inv"])
    return (
        grad_input.reshape(snapshots.shape),
        local_grad.T,
        from_rows(new_weight),
        from_rows(new_first),
        from_rows(new_second),
    )


def solution(mesh):
    tables = make_tables()
    split_spec = P("dp", "grid", None)
    field_spec = P("dp", None, "grid", None, None)

    def step(*args):
        return on_device(tables, *args)

    return jax.shard_map(
        step,
        mesh=mesh,
        in_specs=(field_spec, field_spec, P(), split_spec, split_spec, split_spec),
        out_specs=(field_spec, P(), split_spec, split_spec, split_spec),
        check_vma=False,
    )
```
